256 devices in a mesh: seq: 32 (over z, y), head: 8 (over x, core).
Axes of the slice: x: 4, y: 4, z: 8, core: 2. Of those that a mesh axis runs over, the one named last changes fastest.
Arguments:
- grad_y: bfloat16 [16384, 4096], P('seq', 'head'), may hold values from -6 to 6
- w_out: bfloat16 [4096, 4096], P('head'), may hold values from -0.09375 to 0.09375
- queries: bfloat16 [16384, 4096], P('seq', 'head'), may hold values from -6 to 6
- keys: bfloat16 [16384, 4096], P('seq', 'head'), may hold values from -6 to 6
- values: bfloat16 [16384, 4096], P('seq', 'head'), may hold values from -6 to 6
- level_rows: int32 [16384], P('seq'), may hold values from 0 to 127
- level_table: float32 [128, 12, 32], P(None, None, 'head'), may hold values from 0.2 to 3
Outputs:
- query_grad: float32 [16384, 4096], P('seq', 'head')
- key_grad: float32 [16384, 4096], P('seq', 'head')
- value_grad: float32 [16384, 4096], P('seq', 'head')
The draws below stay inside these ranges and needn't reach their ends.
Inputs may be any that keep to these rules, and one draw needn't show every extreme that they name: `level_rows`: each token names one row of the level-weight table.
All inputs are finite; a program needn't handle non-finite values.
Results may differ from the reference program's by a relative error of at most 0.0049.
Values may be sent and summed in bfloat16 or wider, within the bound.
A program may use at most 128 MiB of HBM per device.

```python
import math
import jax
import jax.numpy as jnp
from jax import lax

D = 4096
H = 32
P_SIZE = 128
BLK = 128
LEVELS = 12
WROWS = 128
TOKENS = 16384


def set_ends(result, key, least, top_value):
    longest = result.shape.index(max(result.shape))
    spots = []
    for shift in (0, 1):
        where = [jax.random.randint(jax.random.fold_in(key, axis), (), 0, length) for axis, length in enumerate(result.shape)]
        where[longest] = (where[longest] + shift) % result.shape[longest]
        spots.append(tuple(where))
    return result.at[spots[0]].set(least).at[spots[1]].set(top_value)


def block_levels(stream_key, extent, shards, least, high):
    def one(dim, parts):
        steps = jax.random.uniform(jax.random.fold_in(jax.random.fold_in(stream_key, 6), dim), (parts,), jnp.float32, least / len(shards), high / len(shards))
        return jnp.repeat(jnp.exp(steps), extent[dim] // parts).reshape((-1,) + (1,) * (len(extent) - dim - 1))

    gain = one(*shards[0])
    for cut in shards[1:]:
        gain = gain * one(*cut)
    return gain


def normal_values(stream_key, shape, scale, limit, pieces=(), kind=jnp.bfloat16):
    entries = scale * jax.random.normal(stream_key, shape, jnp.float32)
    if pieces:
        entries = entries * block_levels(stream_key, shape, pieces, -0.22, 0.18)
    return jnp.clip(entries, -limit, limit).astype(kind)


def setup_inputs(seed: int = 0) -> dict:
    arg_keys = jax.random.split(jax.random.key(seed), 8)
    grad_y = normal_values(arg_keys[0], (TOKENS, D), 1.0, 6.0, ((0, 32), (1, 8)))
    w_out = normal_values(arg_keys[1], (H * P_SIZE, D), D ** -0.5, 0.09375, ((0, 8),))
    queries = normal_values(arg_keys[2], (TOKENS, H * P_SIZE), 1.0, 6.0, ((0, 32), (1, 8)))
    keys = normal_values(arg_keys[3], (TOKENS, H * P_SIZE), 1.0, 6.0, ((0, 32), (1, 8)))
    values = normal_values(arg_keys[4], (TOKENS, H * P_SIZE), 1.0, 6.0, ((0, 32), (1, 8)))
    level_rows = set_ends(jax.random.randint(arg_keys[5], (TOKENS,), 0, WROWS), jax.random.fold_in(arg_keys[5], 1), 0, WROWS - 1).astype(jnp.int32)
    level_table = jnp.clip(jnp.exp(math.log(3.0) - 2.7080502 * jax.random.uniform(arg_keys[6], (WROWS, LEVELS, H), jnp.float32) ** block_levels(arg_keys[6], (WROWS, LEVELS, H), ((2, 8),), -0.2, 0.2)), 0.2, 3.0)
    return {"grad_y": grad_y, "w_out": w_out, "queries": queries, "keys": keys, "values": values, "level_rows": level_rows, "level_table": level_table}


def level_norm(level_count, block_size, head_size):
    level_ids = jnp.arange(level_count, dtype=jnp.int32)
    doubling = jnp.exp2(jnp.maximum(level_ids - 1, 0).astype(jnp.float32))
    return lax.rsqrt(doubling * float(block_size * head_size))

def sibling(states, bit_index):
    block_count = states.shape[0]
    span = 2 ** bit_index
    grouped = states.reshape((block_count // span, span) + states.shape[1:]).sum(axis=1)
    paired = grouped.reshape((block_count // (2 * span), 2) + grouped.shape[1:])[:, ::-1]
    return jnp.repeat(paired.reshape(grouped.shape), span, axis=0)

def settle(array_in):
    return lax.optimization_barrier(array_in.astype(jnp.bfloat16)).astype(jnp.float32)

def head_grads(operands):
    query, key_rows, value_rows, grad_rows, weight = operands
    highest = lax.Precision.HIGHEST
    query_wide = query.astype(jnp.float32)
    key_wide = key_rows.astype(jnp.float32)
    value_wide = value_rows.astype(jnp.float32)
    grad_wide = grad_rows.astype(jnp.float32)
    block_count, block_size, head_size = query.shape
    causal = (jnp.arange(block_size)[:, None] >= jnp.arange(block_size)[None, :]).astype(jnp.float32)
    intra_weight = weight[:, :, 0][:, :, None] * causal[None]
    intra_grad = settle(jnp.einsum('bti,bsi->bts', grad_wide, value_wide, precision=highest) * intra_weight)
    intra_score = settle(jnp.einsum('bti,bsi->bts', query_wide, key_wide, precision=highest) * intra_weight)
    query_grad = jnp.einsum('bts,bsi->bti', intra_grad, key_wide, precision=highest)
    key_grad = jnp.einsum('bts,bti->bsi', intra_grad, query_wide, precision=highest)
    value_grad = jnp.einsum('bts,bti->bsi', intra_score, grad_wide, precision=highest)
    states = jnp.einsum('bsi,bsj->bij', key_wide, value_wide, precision=highest)
    block_ids = jnp.arange(block_count, dtype=jnp.int32)
    adjoint = jnp.zeros_like(states)
    for bit_index in range(block_count.bit_length() - 1):
        present = (block_ids >> bit_index & 1).astype(jnp.float32)[:, None, None]
        bucket = settle(sibling(states, bit_index) * present)
        level_weight = weight[:, :, bit_index + 1][:, :, None]
        query_grad = query_grad + level_weight * jnp.einsum('btj,bij->bti', grad_wide, bucket, precision=highest)
        weighted = settle(level_weight * query_wide)
        adjoint_part = jnp.einsum('bti,btj->bij', weighted, grad_wide, precision=highest) * present
        adjoint = adjoint + sibling(adjoint_part, bit_index)
    adjoint = settle(adjoint)
    key_grad = key_grad + jnp.einsum('bsj,bij->bsi', value_wide, adjoint, precision=highest)
    value_grad = value_grad + jnp.einsum('bsi,bij->bsj', key_wide, adjoint, precision=highest)
    return (query_grad, key_grad, value_grad)

def reference(grad_y, w_out, queries, keys, values, level_rows, level_table):
    token_count, width = queries.shape
    head_count = level_table.shape[2]
    head_size = width // head_count
    level_count = level_table.shape[1]
    block_count = token_count // BLK
    grad_out = jnp.dot(grad_y, w_out.T, preferred_element_type=jnp.float32).astype(jnp.bfloat16)
    weights = level_table[level_rows] * level_norm(level_count, BLK, head_size)[None, :, None]

    def per_head(array_in):
        return array_in.reshape(block_count, BLK, head_count, head_size).transpose(2, 0, 1, 3)
    stacked_weights = weights.reshape(block_count, BLK, level_count, head_count).transpose(3, 0, 1, 2)
    results = lax.map(head_grads, (per_head(queries), per_head(keys), per_head(values), per_head(grad_out), stacked_weights))

    def merged(array_in):
        return array_in.transpose(1, 2, 0, 3).reshape(token_count, width)
    return (merged(results[0]), merged(results[1]), merged(results[2]))
```

```python
import functools

import jax
import jax.numpy as jnp
from jax import lax
from jax.experimental import pallas as pl
from jax.experimental.pallas import tpu as pltpu
from jax.sharding import PartitionSpec as P

BLK = 128
CORES = 2
MESH = pl.DeviceIdType.MESH
NN = (((1,), (0,)), ((), ()))
NT = (((1,), (1,)), ((), ()))
TN = (((0,), (0,)), ((), ()))
F32 = jnp.float32
BF16 = jnp.bfloat16


def dot(a, b, dims=NN):
    return lax.dot_general(a, b, dims, preferred_element_type=F32)


def layer(
    seq_size, head_size, heads,
    y, w, q, k, v, rows, table,
    qg_out, kg_out, vg_out,
    yb, wb, qb, kb, vb, gb, qg, kg, vg,
    wrow, wcol, wq, score, state, local_bucket, local_adjoint,
    total, bucket_in, bucket_sum, bucket,
    part, part_in, part_sum, carried,
    load_sem, own_sem, send_sem, y_sem,
    bs1, br1, bs2, br2, as1, ar1, as2, ar2, out_sem,
):
    tokens, feats = y.shape
    width = heads * BLK
    blocks = tokens // BLK
    local_bits = blocks.bit_length() - 1
    device_bits = seq_size.bit_length() - 1
    levels = 1 + local_bits + device_bits
    ring = head_size // CORES
    pos = lax.axis_index("seq")
    head = lax.axis_index("head")
    x, core = head // CORES, lax.rem(head, CORES)
    right = lax.rem(x + 1, ring) * CORES + core
    left = lax.rem(x + ring - 1, ring) * CORES + core
    across = lax.rem(x + 2, ring) * CORES + core
    twin = x * CORES + 1 - core

    loads = [
        pltpu.make_async_copy(src, dst, load_sem.at[n])
        for n, (src, dst) in enumerate(((k, kb), (v, vb), (q, qb), (w, wb)))
    ]
    for load in loads:
        load.start()

    bucket[...] = jnp.zeros_like(bucket)
    carried[...] = jnp.zeros_like(carried)

    barrier = pltpu.get_barrier_semaphore()

    def greet(step, _):
        peer = lax.rem(pos + step, seq_size)
        pl.semaphore_signal(barrier, inc=1, device_id=(peer, head), device_id_type=MESH)
        return 0

    for peer in (right, left, twin):
        pl.semaphore_signal(barrier, inc=1, device_id=(pos, peer), device_id_type=MESH)
    lax.fori_loop(1, seq_size, greet, 0)
    pl.semaphore_wait(barrier, seq_size - 1 + 3)

    def columns(owner):
        return pl.ds(pl.multiple_of(owner * feats, feats), feats)

    def place(owner, row, count):
        return yb.at[pl.ds(row, count), columns(owner)]

    def send(src, dst, sem_out, sem_in, peer):
        pltpu.make_async_remote_copy(
            src_ref=src, dst_ref=dst, send_sem=sem_out, recv_sem=sem_in,
            device_id=peer, device_id_type=MESH,
        ).start()

    for b in range(blocks):
        src = y.at[pl.ds(b * BLK, BLK), :]
        for n, peer in enumerate((right, left, twin)):
            send(src, place(head, b * BLK, BLK), own_sem.at[n], y_sem.at[head, b], (pos, peer))
        pltpu.make_async_copy(src, place(head, b * BLK, BLK), y_sem.at[head, b]).start()

    def wait_y(owner, b):
        here = place(owner, b * BLK, BLK)
        pltpu.make_async_copy(here, here, y_sem.at[owner, b]).wait()

    half = BLK // 2

    def forward_near(b):
        wait_y(left, b)
        piece = place(left, b * BLK, half)
        send(piece, piece, send_sem.at[0], y_sem.at[left, b], (pos, right))
        piece = place(left, b * BLK, BLK)
        send(piece, piece, send_sem.at[2], y_sem.at[left, b], (pos, twin))
        wait_y(right, b)
        piece = place(right, b * BLK + half, half)
        send(piece, piece, send_sem.at[1], y_sem.at[right, b], (pos, left))
        piece = place(right, b * BLK, BLK)
        send(piece, piece, send_sem.at[3], y_sem.at[right, b], (pos, twin))

    def forward_far(b):
        wait_y(across, b)
        piece = place(across, b * BLK, BLK)
        send(piece, piece, send_sem.at[4], y_sem.at[across, b], (pos, twin))

    def finish_y(b):
        wait_y(head, b)
        wait_y(twin, b)
        for owner in (left, right, across):
            wait_y(owner + 1 - 2 * core, b)

    def project(b):
        at = pl.ds(b * BLK, BLK)
        gb[at, :] = dot(yb[at, :], wb[...], NT).astype(BF16)

    def spans(bit):
        count = 2 << bit
        return count, width // count, lax.rem(pos, count)

    def scatter_rows(bit, src_bit, data, landing, result, sem_out, sem_in, sem_result):
        count, size, index = spans(bit)

        @pl.when(lax.rem(pos // (1 << bit), 2) == src_bit)
        def _():
            if bit == 0:
                send(data, result.at[0], sem_out.at[0], sem_result.at[0], (pos + 1 - 2 * src_bit, head))
                return
            slot = landing.at[bit, pl.ds(pl.multiple_of(lax.rem(index, 1 << bit) * size, size), size), :]

            def step(off, _):
                owner = lax.rem(index + off, count)
                src = data.at[pl.ds(pl.multiple_of(owner * size, size), size), :]
                send(src, slot, sem_out.at[bit], sem_in.at[bit], (pos - index + owner, head))
                return 0

            lax.fori_loop(1, count, step, 0)
            src = data.at[pl.ds(pl.multiple_of(index * size, size), size), :]
            pltpu.make_async_copy(src, slot, sem_in.at[bit]).start()

    def sum_rows(bit, src_bit, landing, summed, result, sem_in, sem_out, sem_result):
        if bit == 0:
            return
        count, size, index = spans(bit)
        here = landing.at[bit]
        pltpu.make_async_copy(here, here, sem_in.at[bit]).wait()
        value = landing[bit, 0:size, :].astype(F32)
        for n in range(1, 1 << bit):
            value = value + landing[bit, n * size:(n + 1) * size, :].astype(F32)
        summed[bit, 0:size, :] = value.astype(BF16)
        src = summed.at[bit, pl.ds(0, size), :]
        dst = result.at[bit, pl.ds(pl.multiple_of(index * size, size), size), :]
        first = (1 - src_bit) * (1 << bit)
        own = lax.rem(index, 1 << bit)
        sink = lax.rem(pos // (1 << bit), 2) != src_bit

        def step(off, _):
            peer = first + lax.rem(own + off, 1 << bit)
            send(src, dst, sem_out.at[bit], sem_result.at[bit], (pos - index + peer, head))
            return 0

        lax.fori_loop(1, 1 << bit, step, 0)

        @pl.when(sink)
        def _():
            pltpu.make_async_copy(src, dst, sem_result.at[bit]).start()

        @pl.when(jnp.logical_not(sink))
        def _():
            step(0, 0)

    def wait_result(bit, src_bit, result, sem_result):
        @pl.when(lax.rem(pos // (1 << bit), 2) != src_bit)
        def _():
            here = result.at[bit]
            pltpu.make_async_copy(here, here, sem_result.at[bit]).wait()

    def drain(bit, src_bit, data, landing, sem_first, sem_second):
        count, size, _ = spans(bit)
        source = lax.rem(pos // (1 << bit), 2) == src_bit

        @pl.when(source)
        def _():
            sent = data if bit == 0 else data.at[pl.ds(0, width - size), :]
            pltpu.make_async_copy(sent, sent, sem_first.at[bit]).wait()
            if bit > 0:
                again = landing.at[bit]
                pltpu.make_async_copy(again, again, sem_second.at[bit]).wait()

        if bit > 0:
            @pl.when(jnp.logical_not(source))
            def _():
                again = landing.at[bit, pl.ds(0, width // 2 - size), :]
                pltpu.make_async_copy(again, again, sem_second.at[bit]).wait()

    loads[0].wait()
    loads[1].wait()
    lanes = [slice(h * BLK, (h + 1) * BLK) for h in range(heads)]
    for h in range(heads):
        sums = jnp.zeros((BLK, BLK), F32)
        for b in range(blocks):
            at = slice(b * BLK, (b + 1) * BLK)
            value = dot(kb[at, lanes[h]], vb[at, lanes[h]], TN)
            state[b, lanes[h], :] = value
            sums = sums + value
        total[lanes[h], :] = sums.astype(BF16)
    for bit in reversed(range(device_bits)):
        scatter_rows(bit, 0, total, bucket_in, bucket, bs1, br1, br2)

    level = lax.rem(lax.broadcasted_iota(jnp.int32, table.shape, 0), levels)
    norm = jnp.zeros(table.shape, F32)
    for n in range(levels):
        norm = jnp.where(level == n, (BLK * BLK * 2.0 ** max(n - 1, 0)) ** -0.5, norm)
    scaled = table[...] * norm
    hot = (lax.broadcasted_iota(jnp.int32, (table.shape[1], tokens), 0) == rows[...]).astype(BF16)
    weight = jnp.zeros((table.shape[0], tokens), F32)
    for _ in range(3):
        piece = scaled.astype(BF16)
        scaled = scaled - piece.astype(F32)
        weight = weight + dot(piece, hot)
    wrow[...] = weight
    padded = jnp.concatenate([weight, jnp.zeros((BLK - weight.shape[0], tokens), F32)], axis=0)
    for b in range(blocks):
        at = slice(b * BLK, (b + 1) * BLK)
        wcol[at, :] = padded[:, at].T

    for m in range(local_bits):
        for b in range(blocks):
            if b >> m & 1:
                first = ((b >> m) ^ 1) << m
                value = state[first]
                for n in range(first + 1, first + (1 << m)):
                    value = value + state[n]
                local_bucket[b, m] = value.astype(BF16)
            else:
                local_bucket[b, m] = jnp.zeros((width, BLK), BF16)

    loads[2].wait()
    row_id = lax.broadcasted_iota(jnp.int32, (BLK, BLK), 0)
    col_id = lax.broadcasted_iota(jnp.int32, (BLK, BLK), 1)
    forward_near(0)
    for h in range(heads):
        for b in range(blocks):
            at = slice(b * BLK, (b + 1) * BLK)
            value = dot(kb[at, lanes[h]], qb[at, lanes[h]], NT)
            value = value * jnp.where(col_id >= row_id, wrow[h * levels:h * levels + 1, at], 0.0)
            score[b, lanes[h], :] = value.astype(BF16)
    forward_near(1)
    for bit in reversed(range(device_bits)):
        sum_rows(bit, 0, bucket_in, bucket_sum, bucket, br1, bs2, br2)
    for h in range(heads):
        for b in range(blocks):
            at = slice(b * BLK, (b + 1) * BLK)
            turned = qb[at, lanes[h]].astype(F32).T
            for n in range(1, levels):
                value = turned * wrow[h * levels + n:h * levels + n + 1, at]
                wq[h, (n - 1) * BLK:n * BLK, at] = value.astype(BF16)
    forward_near(2)
    forward_far(0)
    loads[3].wait()
    finish_y(0)
    project(0)
    forward_near(3)
    forward_far(1)
    finish_y(1)
    project(1)
    forward_far(2)
    finish_y(2)
    project(2)
    forward_far(3)
    finish_y(3)
    project(3)

    for h in range(heads):
        for bit in range(device_bits):
            n = local_bits + bit
            value = dot(wq[h, n * BLK:(n + 1) * BLK, :], gb[:, lanes[h]])
            part[bit, lanes[h], :] = value.astype(BF16)
    for bit in reversed(range(device_bits)):
        scatter_rows(bit, 1, part.at[bit], part_in, carried, as1, ar1, ar2)

    for h in range(heads):
        sums = [jnp.zeros((BLK, BLK), F32) for _ in range(blocks)]
        for m in range(local_bits):
            for u in range(1, blocks >> m, 2):
                at = slice(u << m << 7, (u + 1) << m << 7)
                value = dot(wq[h, m * BLK:(m + 1) * BLK, at], gb[at, lanes[h]])
                for j in range((u - 1) << m, u << m):
                    sums[j] = sums[j] + value
        for j in range(blocks):
            local_adjoint[j, lanes[h], :] = sums[j]

    def inner(b, _):
        at = pl.ds(pl.multiple_of(b * BLK, BLK), BLK)
        for h in range(heads):
            grad, key = gb[at, lanes[h]], kb[at, lanes[h]]
            value = dot(grad, vb[at, lanes[h]], NT)
            value = jnp.where(row_id >= col_id, value * wcol[at, h * levels:h * levels + 1], 0.0)
            intra = value.astype(BF16)
            kg[at, lanes[h]] = dot(intra, qb[at, lanes[h]], TN)
            vg[at, lanes[h]] = dot(score[b, lanes[h], :], grad)
            value = dot(intra, key)
            for m in range(local_bits):
                n = h * levels + 1 + m
                value = value + wcol[at, n:n + 1] * dot(grad, local_bucket[b, m, lanes[h], :], NT)
            qg[at, lanes[h]] = value
        return 0

    lax.fori_loop(0, blocks, inner, 0)
    for bit in reversed(range(device_bits)):
        sum_rows(bit, 1, part_in, part_sum, carried, ar1, as2, ar2)
    for bit in range(device_bits):
        wait_result(bit, 0, bucket, br2)

    def outer(b, _):
        at = pl.ds(pl.multiple_of(b * BLK, BLK), BLK)
        for h in range(heads):
            grad = gb[at, lanes[h]]
            value = qg[at, lanes[h]]
            for bit in range(device_bits):
                n = h * levels + 1 + local_bits + bit
                value = value + wcol[at, n:n + 1] * dot(grad, bucket[bit, lanes[h], :], NT)
            qg[at, lanes[h]] = value
        return 0

    lax.fori_loop(0, blocks, outer, 0)
    out_q = pltpu.make_async_copy(qg, qg_out, out_sem.at[0])
    out_q.start()

    for bit in range(device_bits):
        wait_result(bit, 1, carried, ar2)
    for h in range(heads):
        sums = carried[0, lanes[h], :].astype(F32)
        for bit in range(1, device_bits):
            sums = sums + carried[bit, lanes[h], :].astype(F32)
        for b in range(blocks):
            at = slice(b * BLK, (b + 1) * BLK)
            adjoint = (local_adjoint[b, lanes[h], :] + sums).astype(BF16)
            kg[at, lanes[h]] += dot(vb[at, lanes[h]], adjoint, NT)
            vg[at, lanes[h]] += dot(kb[at, lanes[h]], adjoint)
    out_k = pltpu.make_async_copy(kg, kg_out, out_sem.at[1])
    out_v = pltpu.make_async_copy(vg, vg_out, out_sem.at[2])
    out_k.start()
    out_v.start()

    for bit in range(device_bits):
        drain(bit, 0, total, bucket_in, bs1, bs2)
        drain(bit, 1, part.at[bit], part_in, as1, as2)
    for n in range(3):
        pltpu.make_async_copy(y, y, own_sem.at[n]).wait()
    for n in range(5):
        sent = yb.at[pl.ds(0, tokens // 2 if n < 2 else tokens), pl.ds(0, feats)]
        pltpu.make_async_copy(sent, sent, send_sem.at[n]).wait()
    out_q.wait()
    out_k.wait()
    out_v.wait()


def shards(grad_y, w_out, queries, keys, values, level_rows, level_table):
    tokens, width = queries.shape
    feats = grad_y.shape[1]
    heads = level_table.shape[2]
    blocks = tokens // BLK
    seq_size, head_size = lax.axis_size("seq"), lax.axis_size("head")
    device_bits = seq_size.bit_length() - 1
    local_bits = blocks.bit_length() - 1
    levels = 1 + local_bits + device_bits
    table = level_table[:, :levels, :].transpose(2, 1, 0).reshape(heads * levels, level_table.shape[0])
    hbm = pl.BlockSpec(memory_space=pl.ANY)
    vmem = pl.BlockSpec(memory_space=pltpu.VMEM)
    dma = pltpu.SemaphoreType.DMA
    tree = [
        pltpu.VMEM((device_bits, width // 2, BLK), BF16),
        pltpu.VMEM((device_bits, width // 4, BLK), BF16),
        pltpu.VMEM((device_bits, width, BLK), BF16),
    ]
    out = jax.ShapeDtypeStruct((tokens, width), F32)
    return pl.pallas_call(
        functools.partial(layer, seq_size, head_size, heads),
        out_shape=(out, out, out),
        in_specs=[hbm] * 5 + [vmem] * 2,
        out_specs=(hbm,) * 3,
        scratch_shapes=[
            pltpu.VMEM((tokens, head_size * feats), BF16),
            pltpu.VMEM(w_out.shape, BF16),
            pltpu.VMEM((tokens, width), BF16),
            pltpu.VMEM((tokens, width), BF16),
            pltpu.VMEM((tokens, width), BF16),
            pltpu.VMEM((tokens, width), BF16),
            pltpu.VMEM((tokens, width), F32),
            pltpu.VMEM((tokens, width), F32),
            pltpu.VMEM((tokens, width), F32),
            pltpu.VMEM((heads * levels, tokens), F32),
            pltpu.VMEM((tokens, BLK), F32),
            pltpu.VMEM((heads, (levels - 1) * BLK, tokens), BF16),
            pltpu.VMEM((blocks, width, BLK), BF16),
            pltpu.VMEM((blocks, width, BLK), F32),
            pltpu.VMEM((blocks, local_bits, width, BLK), BF16),
            pltpu.VMEM((blocks, width, BLK), F32),
            pltpu.VMEM((width, BLK), BF16),
            *tree,
            pltpu.VMEM((device_bits, width, BLK), BF16),
            *tree,
            dma((4,)),
            dma((3,)),
            dma((5,)),
            dma((head_size, blocks)),
            *[dma((device_bits,))] * 8,
            dma((3,)),
        ],
        compiler_params=pltpu.CompilerParams(
            collective_id=0, has_side_effects=True, vmem_limit_bytes=56 * 2**20
        ),
        name="layer",
    )(grad_y, w_out, queries, keys, values, level_rows.reshape(1, tokens), table)


def solution(mesh):
    return jax.shard_map(
        shards,
        mesh=mesh,
        in_specs=(
            P("seq", "head"),
            P("head", None),
            P("seq", "head"),
            P("seq", "head"),
            P("seq", "head"),
            P("seq"),
            P(None, None, "head"),
        ),
        out_specs=(P("seq", "head"), P("seq", "head"), P("seq", "head")),
        check_vma=False,
    )
```

```python
import functools

import jax
import jax.numpy as jnp
from jax import lax
from jax.experimental import pallas as pl
from jax.experimental.pallas import tpu as pltpu
from jax.sharding import PartitionSpec as P

BLK = 128
CORES = 2
MESH = pl.DeviceIdType.MESH
NN = (((1,), (0,)), ((), ()))
NT = (((1,), (1,)), ((), ()))
TN = (((0,), (0,)), ((), ()))
F32 = jnp.float32
BF16 = jnp.bfloat16


def dot(a, b, dims=NN):
    return lax.dot_general(a, b, dims, preferred_element_type=F32)


def layer(
    seq_size, head_size, heads,
    y, w, q, k, v, rows, table,
    qg, kg, vg,
    yb, wb, qb, kb, vb, gb, near, levels_in, scaled_levels,
    wrow, wcol, wq, score, state, local_bucket, local_adjoint,
    total, bucket_in, bucket_sum, bucket,
    part, part_early, part_in, part_sum, carried,
    load_sem, own_sem, send_sem, y_sem,
    bs1, br1, bs2, br2, as1, ar1, as2, ar2
):
    tokens, feats = y.shape
    width = heads * BLK
    blocks = tokens // BLK
    local_bits = blocks.bit_length() - 1
    device_bits = seq_size.bit_length() - 1
    levels = 1 + local_bits + device_bits
    ring = head_size // CORES
    pos = lax.axis_index("seq")
    head = lax.axis_index("head")
    x, core = head // CORES, lax.rem(head, CORES)
    right = lax.rem(x + 1, ring) * CORES + core
    left = lax.rem(x + ring - 1, ring) * CORES + core
    across = lax.rem(x + 2, ring) * CORES + core
    near_chips, far_chip = (x, lax.rem(x + 1, ring), lax.rem(x + ring - 1, ring)), lax.rem(x + 2, ring)
    twin = x * CORES + 1 - core

    loads = [
        pltpu.make_async_copy(src, dst, load_sem.at[n])
        for n, (src, dst) in enumerate(((k, kb), (v, vb), (table, levels_in), (q, qb), (w, wb)))
    ]
    for load in loads:
        load.start()

    bucket[...] = jnp.zeros_like(bucket)
    carried[...] = jnp.zeros_like(carried)

    barrier = pltpu.get_barrier_semaphore()

    def greet(step, _):
        peer = lax.rem(pos + step, seq_size)
        pl.semaphore_signal(barrier, inc=1, device_id=(peer, head), device_id_type=MESH)
        return 0

    for peer in (right, left, twin):
        pl.semaphore_signal(barrier, inc=1, device_id=(pos, peer), device_id_type=MESH)
    lax.fori_loop(1, seq_size, greet, 0)
    pl.semaphore_wait(barrier, seq_size - 1 + 3)

    def columns(owner):
        return pl.ds(pl.multiple_of(owner * feats, feats), feats)

    def place(owner, row, count):
        return yb.at[pl.ds(row, count), columns(owner)]

    def send(src, dst, sem_out, sem_in, peer):
        pltpu.make_async_remote_copy(
            src_ref=src, dst_ref=dst, send_sem=sem_out, recv_sem=sem_in,
            device_id=peer, device_id_type=MESH,
        ).start()

    for b in range(blocks):
        src = y.at[pl.ds(b * BLK, BLK), :]
        for n, peer in enumerate((right, left, twin)):
            send(src, place(head, b * BLK, BLK), own_sem.at[n], y_sem.at[head, b], (pos, peer))
        pltpu.make_async_copy(src, place(head, b * BLK, BLK), y_sem.at[head, b]).start()

    def wait_y(owner, b):
        here = place(owner, b * BLK, BLK)
        pltpu.make_async_copy(here, here, y_sem.at[owner, b]).wait()

    half = BLK // 2

    def forward_near(b):
        wait_y(left, b)
        piece = place(left, b * BLK, half)
        send(piece, piece, send_sem.at[0], y_sem.at[left, b], (pos, right))
        piece = place(left, b * BLK, BLK)
        send(piece, piece, send_sem.at[2], y_sem.at[left, b], (pos, twin))
        wait_y(right, b)
        piece = place(right, b * BLK + half, half)
        send(piece, piece, send_sem.at[1], y_sem.at[right, b], (pos, left))
        piece = place(right, b * BLK, BLK)
        send(piece, piece, send_sem.at[3], y_sem.at[right, b], (pos, twin))

    def forward_far(b):
        wait_y(across, b)
        piece = place(across, b * BLK, BLK)
        send(piece, piece, send_sem.at[4], y_sem.at[across, b], (pos, twin))

    def take_twin(owners, b):
        for owner in owners:
            wait_y(owner + 1 - 2 * core, b)

    def product(at, chip):
        inner = pl.ds(pl.multiple_of(chip * CORES * feats, CORES * feats), CORES * feats)
        return dot(yb[at, inner], wb[:, inner], NT)

    def project_near(b, count):
        for n in range(b, b + count):
            wait_y(head, n)
            take_twin((head, left, right), n)
        at = pl.ds(b * BLK, count * BLK)
        value = product(at, near_chips[0])
        for chip in near_chips[1:]:
            value = value + product(at, chip)
        near[at, :] = value

    def project_far(b):
        take_twin((across,), b)
        at = pl.ds(b * BLK, BLK)
        gb[at, :] = (near[at, :] + product(at, far_chip)).astype(BF16)

    def spans(bit):
        count = 2 << bit
        return count, width // count, lax.rem(pos, count)

    def scatter_rows(bit, src_bit, data, landing, result, sem_out, sem_in, sem_result):
        count, size, index = spans(bit)

        @pl.when(lax.rem(pos // (1 << bit), 2) == src_bit)
        def _():
            if bit == 0:
                send(data, result.at[0], sem_out.at[0], sem_result.at[0], (pos + 1 - 2 * src_bit, head))
                return
            slot = landing.at[bit, pl.ds(pl.multiple_of(lax.rem(index, 1 << bit) * size, size), size), :]

            def step(off, _):
                owner = lax.rem(index + off, count)
                src = data.at[pl.ds(pl.multiple_of(owner * size, size), size), :]
                send(src, slot, sem_out.at[bit], sem_in.at[bit], (pos - index + owner, head))
                return 0

            lax.fori_loop(1, count, step, 0)
            src = data.at[pl.ds(pl.multiple_of(index * size, size), size), :]
            pltpu.make_async_copy(src, slot, sem_in.at[bit]).start()

    def sum_rows(bit, src_bit, landing, summed, result, sem_in, sem_out, sem_result):
        if bit == 0:
            return
        count, size, index = spans(bit)
        here = landing.at[bit]
        pltpu.make_async_copy(here, here, sem_in.at[bit]).wait()
        value = landing[bit, 0:size, :].astype(F32)
        for n in range(1, 1 << bit):
            value = value + landing[bit, n * size:(n + 1) * size, :].astype(F32)
        summed[bit, 0:size, :] = value.astype(BF16)
        src = summed.at[bit, pl.ds(0, size), :]
        dst = result.at[bit, pl.ds(pl.multiple_of(index * size, size), size), :]
        first = (1 - src_bit) * (1 << bit)
        own = lax.rem(index, 1 << bit)
        sink = lax.rem(pos // (1 << bit), 2) != src_bit

        def step(off, _):
            peer = first + lax.rem(own + off, 1 << bit)
            send(src, dst, sem_out.at[bit], sem_result.at[bit], (pos - index + peer, head))
            return 0

        lax.fori_loop(1, 1 << bit, step, 0)

        @pl.when(sink)
        def _():
            pltpu.make_async_copy(src, dst, sem_result.at[bit]).start()

        @pl.when(jnp.logical_not(sink))
        def _():
            step(0, 0)

    def wait_result(bit, src_bit, result, sem_result):
        @pl.when(lax.rem(pos // (1 << bit), 2) != src_bit)
        def _():
            here = result.at[bit]
            pltpu.make_async_copy(here, here, sem_result.at[bit]).wait()

    def drain(bit, src_bit, data, landing, sem_first, sem_second):
        count, size, _ = spans(bit)
        source = lax.rem(pos // (1 << bit), 2) == src_bit

        @pl.when(source)
        def _():
            sent = data if bit == 0 else data.at[pl.ds(0, width - size), :]
            pltpu.make_async_copy(sent, sent, sem_first.at[bit]).wait()
            if bit > 0:
                again = landing.at[bit]
                pltpu.make_async_copy(again, again, sem_second.at[bit]).wait()

        if bit > 0:
            @pl.when(jnp.logical_not(source))
            def _():
                again = landing.at[bit, pl.ds(0, width // 2 - size), :]
                pltpu.make_async_copy(again, again, sem_second.at[bit]).wait()

    loads[0].wait()
    loads[1].wait()
    lanes = [slice(h * BLK, (h + 1) * BLK) for h in range(heads)]
    for h in range(heads):
        sums = jnp.zeros((BLK, BLK), F32)
        for b in range(blocks):
            at = slice(b * BLK, (b + 1) * BLK)
            value = dot(kb[at, lanes[h]], vb[at, lanes[h]], TN)
            state[b, lanes[h], :] = value
            sums = sums + value
        total[lanes[h], :] = sums.astype(BF16)
    for bit in reversed(range(device_bits)):
        scatter_rows(bit, 0, total, bucket_in, bucket, bs1, br1, br2)

    loads[2].wait()
    for n in range(levels):
        scale = (BLK * BLK * 2.0 ** max(n - 1, 0)) ** -0.5
        scaled_levels[n * heads:(n + 1) * heads, :] = levels_in[n] * scale
    scaled = scaled_levels[...]
    hot = (lax.broadcasted_iota(jnp.int32, (scaled.shape[1], tokens), 0) == rows[...]).astype(BF16)
    weight = jnp.zeros((scaled.shape[0], tokens), F32)
    for _ in range(3):
        piece = scaled.astype(BF16)
        scaled = scaled - piece.astype(F32)
        weight = weight + dot(piece, hot)
    wrow[...] = weight
    padded = jnp.concatenate([weight, jnp.zeros((BLK - weight.shape[0], tokens), F32)], axis=0)
    for b in range(blocks):
        at = slice(b * BLK, (b + 1) * BLK)
        wcol[at, :] = padded[:, at].T

    for m in range(local_bits):
        for b in range(blocks):
            if b >> m & 1:
                first = ((b >> m) ^ 1) << m
                value = state[first]
                for n in range(first + 1, first + (1 << m)):
                    value = value + state[n]
                local_bucket[b, m] = value.astype(BF16)
            else:
                local_bucket[b, m] = jnp.zeros((width, BLK), BF16)

    loads[3].wait()
    row_id = lax.broadcasted_iota(jnp.int32, (BLK, BLK), 0)
    col_id = lax.broadcasted_iota(jnp.int32, (BLK, BLK), 1)
    forward_near(0)
    for h in range(heads):
        for b in range(blocks):
            at = slice(b * BLK, (b + 1) * BLK)
            value = dot(kb[at, lanes[h]], qb[at, lanes[h]], NT)
            value = value * jnp.where(col_id >= row_id, wrow[h:h + 1, at], 0.0)
            score[b, lanes[h], :] = value.astype(BF16)
    forward_near(1)
    for bit in reversed(range(device_bits)):
        sum_rows(bit, 0, bucket_in, bucket_sum, bucket, br1, bs2, br2)
    for h in range(heads):
        for b in range(blocks):
            at = slice(b * BLK, (b + 1) * BLK)
            turned = qb[at, lanes[h]].astype(F32).T
            for n in range(1, levels):
                value = turned * wrow[n * heads + h:n * heads + h + 1, at]
                wq[h, (n - 1) * BLK:n * BLK, at] = value.astype(BF16)
    forward_near(2)
    loads[4].wait()
    pair = blocks // 2
    project_near(0, pair)
    for b in range(3, blocks):
        forward_near(b)
    forward_far(0)
    project_near(pair, blocks - pair)

    early = slice(0, pair * BLK)
    late = slice(pair * BLK, tokens)
    for b in range(1, blocks):
        forward_far(b)
        project_far(b - 1)
        if b == pair:
            for h in range(heads):
                for bit in range(device_bits):
                    n = local_bits + bit
                    part_early[bit, lanes[h], :] = dot(wq[h, n * BLK:(n + 1) * BLK, early], gb[early, lanes[h]])
    project_far(blocks - 1)

    for bit in reversed(range(device_bits)):
        n = local_bits + bit
        for h in range(heads):
            value = part_early[bit, lanes[h], :] + dot(wq[h, n * BLK:(n + 1) * BLK, late], gb[late, lanes[h]])
            part[bit, lanes[h], :] = value.astype(BF16)
        scatter_rows(bit, 1, part.at[bit], part_in, carried, as1, ar1, ar2)

    for h in range(heads):
        sums = [jnp.zeros((BLK, BLK), F32) for _ in range(blocks)]
        for m in range(local_bits):
            for u in range(1, blocks >> m, 2):
                at = slice(u << m << 7, (u + 1) << m << 7)
                value = dot(wq[h, m * BLK:(m + 1) * BLK, at], gb[at, lanes[h]])
                for j in range((u - 1) << m, u << m):
                    sums[j] = sums[j] + value
        for j in range(blocks):
            local_adjoint[j, lanes[h], :] = sums[j]

    def inner(b, _):
        at = pl.ds(pl.multiple_of(b * BLK, BLK), BLK)
        for h in range(heads):
            grad, key = gb[at, lanes[h]], kb[at, lanes[h]]
            value = dot(grad, vb[at, lanes[h]], NT)
            value = jnp.where(row_id >= col_id, value * wcol[at, h:h + 1], 0.0)
            intra = value.astype(BF16)
            kg[at, lanes[h]] = dot(intra, qb[at, lanes[h]], TN)
            vg[at, lanes[h]] = dot(score[b, lanes[h], :], grad)
            value = dot(intra, key)
            for m in range(local_bits):
                n = (1 + m) * heads + h
                value = value + wcol[at, n:n + 1] * dot(grad, local_bucket[b, m, lanes[h], :], NT)
            qg[at, lanes[h]] = value
        return 0

    lax.fori_loop(0, blocks, inner, 0)
    for bit in reversed(range(device_bits)):
        sum_rows(bit, 1, part_in, part_sum, carried, ar1, as2, ar2)
    for bit in range(device_bits):
        wait_result(bit, 0, bucket, br2)

    def outer(b, _):
        at = pl.ds(pl.multiple_of(b * BLK, BLK), BLK)
        for h in range(heads):
            grad = gb[at, lanes[h]]
            value = qg[at, lanes[h]]
            for bit in range(device_bits):
                n = (1 + local_bits + bit) * heads + h
                value = value + wcol[at, n:n + 1] * dot(grad, bucket[bit, lanes[h], :], NT)
            qg[at, lanes[h]] = value
        return 0

    lax.fori_loop(0, blocks, outer, 0)

    for bit in range(device_bits):
        wait_result(bit, 1, carried, ar2)
    for h in range(heads):
        sums = carried[0, lanes[h], :].astype(F32)
        for bit in range(1, device_bits):
            sums = sums + carried[bit, lanes[h], :].astype(F32)
        for b in range(blocks):
            at = slice(b * BLK, (b + 1) * BLK)
            adjoint = (local_adjoint[b, lanes[h], :] + sums).astype(BF16)
            kg[at, lanes[h]] += dot(vb[at, lanes[h]], adjoint, NT)
            vg[at, lanes[h]] += dot(kb[at, lanes[h]], adjoint)

    for bit in range(device_bits):
        drain(bit, 0, total, bucket_in, bs1, bs2)
        drain(bit, 1, part.at[bit], part_in, as1, as2)
    for n in range(3):
        pltpu.make_async_copy(y, y, own_sem.at[n]).wait()
    for n in range(5):
        sent = yb.at[pl.ds(0, tokens // 2 if n < 2 else tokens), pl.ds(0, feats)]
        pltpu.make_async_copy(sent, sent, send_sem.at[n]).wait()


def store(qg, kg, vg, qg_out, kg_out, vg_out, sem):
    copies = [
        pltpu.make_async_copy(src, dst, sem.at[n])
        for n, (src, dst) in enumerate(((qg, qg_out), (kg, kg_out), (vg, vg_out)))
    ]
    for copy in copies:
        copy.start()
    for copy in copies:
        copy.wait()


def shards(grad_y, w_out, queries, keys, values, level_rows, level_table):
    tokens, width = queries.shape
    feats = grad_y.shape[1]
    heads = level_table.shape[2]
    blocks = tokens // BLK
    seq_size, head_size = lax.axis_size("seq"), lax.axis_size("head")
    device_bits = seq_size.bit_length() - 1
    local_bits = blocks.bit_length() - 1
    levels = 1 + local_bits + device_bits
    hbm = pl.BlockSpec(memory_space=pl.ANY)
    vmem = pl.BlockSpec(memory_space=pltpu.VMEM)
    dma = pltpu.SemaphoreType.DMA
    tree = [
        pltpu.VMEM((device_bits, width // 2, BLK), BF16),
        pltpu.VMEM((device_bits, width // 4, BLK), BF16),
        pltpu.VMEM((device_bits, width, BLK), BF16),
    ]
    table = level_table.transpose(1, 2, 0)
    grads = pl.pallas_call(
        functools.partial(layer, seq_size, head_size, heads),
        out_shape=(pltpu.VMEM((tokens, width), F32),) * 3,
        in_specs=[hbm] * 5 + [vmem, hbm],
        out_specs=(vmem,) * 3,
        scratch_shapes=[
            pltpu.VMEM((tokens, head_size * feats), BF16),
            pltpu.VMEM(w_out.shape, BF16),
            pltpu.VMEM((tokens, width), BF16),
            pltpu.VMEM((tokens, width), BF16),
            pltpu.VMEM((tokens, width), BF16),
            pltpu.VMEM((tokens, width), BF16),
            pltpu.VMEM((tokens, width), F32),
            pltpu.VMEM(table.shape, F32),
            pltpu.VMEM((levels * heads, table.shape[2]), F32),
            pltpu.VMEM((heads * levels, tokens), F32),
            pltpu.VMEM((tokens, BLK), F32),
            pltpu.VMEM((heads, (levels - 1) * BLK, tokens), BF16),
            pltpu.VMEM((blocks, width, BLK), BF16),
            pltpu.VMEM((blocks, width, BLK), F32),
            pltpu.VMEM((blocks, local_bits, width, BLK), BF16),
            pltpu.VMEM((blocks, width, BLK), F32),
            pltpu.VMEM((width, BLK), BF16),
            *tree,
            pltpu.VMEM((device_bits, width, BLK), BF16),
            pltpu.VMEM((device_bits, width, BLK), F32),
            *tree,
            dma((5,)),
            dma((3,)),
            dma((5,)),
            dma((head_size, blocks)),
            *[dma((device_bits,))] * 8,
        ],
        compiler_params=pltpu.CompilerParams(
            collective_id=0, has_side_effects=True, vmem_limit_bytes=56 * 2**20
        ),
        name="layer",
    )(grad_y, w_out, queries, keys, values, level_rows.reshape(1, tokens), table)

    return pl.pallas_call(
        store,
        out_shape=(jax.ShapeDtypeStruct((tokens, width), F32),) * 3,
        in_specs=[hbm] * 3,
        out_specs=(hbm,) * 3,
        scratch_shapes=[dma((3,))],
        name="store",
    )(*[pltpu.with_memory_space_constraint(grad, pltpu.VMEM) for grad in grads])


def solution(mesh):
    return jax.shard_map(
        shards,
        mesh=mesh,
        in_specs=(
            P("seq", "head"),
            P("head", None),
            P("seq", "head"),
            P("seq", "head"),
            P("seq", "head"),
            P("seq"),
            P(None, None, "head"),
        ),
        out_specs=(P("seq", "head"), P("seq", "head"), P("seq", "head")),
        check_vma=False,
    )
```

```python
import functools

import jax
import jax.numpy as jnp
from jax import lax
from jax.experimental import pallas as pl
from jax.experimental.pallas import tpu as pltpu
from jax.sharding import PartitionSpec as P

BLK = 128
CORES = 2
MESH = pl.DeviceIdType.MESH
NN = (((1,), (0,)), ((), ()))
NT = (((1,), (1,)), ((), ()))
TN = (((0,), (0,)), ((), ()))
F32 = jnp.float32
BF16 = jnp.bfloat16


def dot(a, b, dims=NN):
    return lax.dot_general(a, b, dims, preferred_element_type=F32)


def layer(
    seq_size, head_size, heads,
    y, w, q, k, v, rows, table,
    qg, kg, vg, kb, vb, local_adjoint, carried,
    yb, wb, qb, gb, near, levels_in, scaled_levels,
    wrow, wcol, wq, score, state, local_bucket,
    total, bucket_in, bucket_sum, bucket,
    part, part_early, part_in, part_sum,
    load_sem, own_sem, send_sem, y_sem,
    bs1, br1, bs2, br2, as1, ar1, as2, ar2
):
    tokens, feats = y.shape
    width = heads * BLK
    blocks = tokens // BLK
    local_bits = blocks.bit_length() - 1
    device_bits = seq_size.bit_length() - 1
    levels = 1 + local_bits + device_bits
    ring = head_size // CORES
    pos = lax.axis_index("seq")
    head = lax.axis_index("head")
    x, core = head // CORES, lax.rem(head, CORES)
    right = lax.rem(x + 1, ring) * CORES + core
    left = lax.rem(x + ring - 1, ring) * CORES + core
    across = lax.rem(x + 2, ring) * CORES + core
    near_chips, far_chip = (x, lax.rem(x + 1, ring), lax.rem(x + ring - 1, ring)), lax.rem(x + 2, ring)
    twin = x * CORES + 1 - core

    loads = [
        pltpu.make_async_copy(src, dst, load_sem.at[n])
        for n, (src, dst) in enumerate(((k, kb), (v, vb), (table, levels_in), (q, qb), (w, wb)))
    ]
    for load in loads:
        load.start()

    barrier = pltpu.get_barrier_semaphore()

    def greet(step, _):
        peer = lax.rem(pos + step, seq_size)
        pl.semaphore_signal(barrier, inc=1, device_id=(peer, head), device_id_type=MESH)
        return 0

    for peer in (right, left, twin):
        pl.semaphore_signal(barrier, inc=1, device_id=(pos, peer), device_id_type=MESH)
    lax.fori_loop(1, seq_size, greet, 0, unroll=True)
    pl.semaphore_wait(barrier, seq_size - 1 + 3)

    def columns(owner):
        return pl.ds(pl.multiple_of(owner * feats, feats), feats)

    def place(owner, row, count):
        return yb.at[pl.ds(row, count), columns(owner)]

    def send(src, dst, sem_out, sem_in, peer):
        pltpu.make_async_remote_copy(
            src_ref=src, dst_ref=dst, send_sem=sem_out, recv_sem=sem_in,
            device_id=peer, device_id_type=MESH,
        ).start()

    for b in range(blocks):
        src = y.at[pl.ds(b * BLK, BLK), :]
        for n, peer in enumerate((right, left, twin)):
            send(src, place(head, b * BLK, BLK), own_sem.at[n], y_sem.at[head, b], (pos, peer))
        pltpu.make_async_copy(src, place(head, b * BLK, BLK), y_sem.at[head, b]).start()

    def wait_y(owner, b):
        here = place(owner, b * BLK, BLK)
        pltpu.make_async_copy(here, here, y_sem.at[owner, b]).wait()

    for bit in range(device_bits):
        has = lax.rem(pos // (1 << bit), 2)

        @pl.when(has == 0)
        def _():
            bucket[bit] = jnp.zeros((width, BLK), BF16)

        @pl.when(has == 1)
        def _():
            carried[bit] = jnp.zeros((width, BLK), BF16)

    half = BLK // 2

    def forward_near(b):
        wait_y(left, b)
        piece = place(left, b * BLK, half)
        send(piece, piece, send_sem.at[0], y_sem.at[left, b], (pos, right))
        piece = place(left, b * BLK, BLK)
        send(piece, piece, send_sem.at[2], y_sem.at[left, b], (pos, twin))
        wait_y(right, b)
        piece = place(right, b * BLK + half, half)
        send(piece, piece, send_sem.at[1], y_sem.at[right, b], (pos, left))
        piece = place(right, b * BLK, BLK)
        send(piece, piece, send_sem.at[3], y_sem.at[right, b], (pos, twin))

    def forward_far(b):
        wait_y(across, b)
        piece = place(across, b * BLK, BLK)
        send(piece, piece, send_sem.at[4], y_sem.at[across, b], (pos, twin))

    def take_twin(owners, b):
        for owner in owners:
            wait_y(owner + 1 - 2 * core, b)

    def product(at, chip):
        inner = pl.ds(pl.multiple_of(chip * CORES * feats, CORES * feats), CORES * feats)
        return dot(yb[at, inner], wb[:, inner], NT)

    def project_near(b, count):
        for n in range(b, b + count):
            wait_y(head, n)
            take_twin((head, left, right), n)
        at = pl.ds(b * BLK, count * BLK)
        value = product(at, near_chips[0])
        for chip in near_chips[1:]:
            value = value + product(at, chip)
        near[at, :] = value

    def project_far(b):
        take_twin((across,), b)
        at = pl.ds(b * BLK, BLK)
        gb[at, :] = (near[at, :] + product(at, far_chip)).astype(BF16)

    def spans(bit):
        count = 2 << bit
        return count, width // count, lax.rem(pos, count)

    def scatter_rows(bit, src_bit, data, landing, result, sem_out, sem_in, sem_result):
        count, size, index = spans(bit)

        @pl.when(lax.rem(pos // (1 << bit), 2) == src_bit)
        def _():
            if bit == 0:
                send(data, result.at[0], sem_out.at[0], sem_result.at[0], (pos + 1 - 2 * src_bit, head))
                return
            slot = landing.at[bit, pl.ds(pl.multiple_of(lax.rem(index, 1 << bit) * size, size), size), :]

            def step(off, _):
                owner = lax.rem(index + off, count)
                src = data.at[pl.ds(pl.multiple_of(owner * size, size), size), :]
                send(src, slot, sem_out.at[bit], sem_in.at[bit], (pos - index + owner, head))
                return 0

            lax.fori_loop(1, count, step, 0)
            src = data.at[pl.ds(pl.multiple_of(index * size, size), size), :]
            pltpu.make_async_copy(src, slot, sem_in.at[bit]).start()

    def sum_rows(bit, src_bit, landing, summed, result, sem_in, sem_out, sem_result):
        if bit == 0:
            return
        count, size, index = spans(bit)
        here = landing.at[bit]
        pltpu.make_async_copy(here, here, sem_in.at[bit]).wait()
        value = landing[bit, 0:size, :].astype(F32)
        for n in range(1, 1 << bit):
            value = value + landing[bit, n * size:(n + 1) * size, :].astype(F32)
        summed[bit, 0:size, :] = value.astype(BF16)
        src = summed.at[bit, pl.ds(0, size), :]
        dst = result.at[bit, pl.ds(pl.multiple_of(index * size, size), size), :]
        first = (1 - src_bit) * (1 << bit)
        own = lax.rem(index, 1 << bit)
        sink = lax.rem(pos // (1 << bit), 2) != src_bit

        def step(off, _):
            peer = first + lax.rem(own + off, 1 << bit)
            send(src, dst, sem_out.at[bit], sem_result.at[bit], (pos - index + peer, head))
            return 0

        lax.fori_loop(1, 1 << bit, step, 0)

        @pl.when(sink)
        def _():
            pltpu.make_async_copy(src, dst, sem_result.at[bit]).start()

        @pl.when(jnp.logical_not(sink))
        def _():
            step(0, 0)

    def wait_result(bit, src_bit, result, sem_result):
        @pl.when(lax.rem(pos // (1 << bit), 2) != src_bit)
        def _():
            here = result.at[bit]
            pltpu.make_async_copy(here, here, sem_result.at[bit]).wait()

    def drain(bit, src_bit, data, landing, sem_first, sem_second):
        count, size, _ = spans(bit)
        source = lax.rem(pos // (1 << bit), 2) == src_bit

        @pl.when(source)
        def _():
            sent = data if bit == 0 else data.at[pl.ds(0, width - size), :]
            pltpu.make_async_copy(sent, sent, sem_first.at[bit]).wait()
            if bit > 0:
                again = landing.at[bit]
                pltpu.make_async_copy(again, again, sem_second.at[bit]).wait()

        if bit > 0:
            @pl.when(jnp.logical_not(source))
            def _():
                again = landing.at[bit, pl.ds(0, width // 2 - size), :]
                pltpu.make_async_copy(again, again, sem_second.at[bit]).wait()

    loads[0].wait()
    loads[1].wait()
    lanes = [slice(h * BLK, (h + 1) * BLK) for h in range(heads)]
    for h in range(heads):
        sums = jnp.zeros((BLK, BLK), F32)
        for b in range(blocks):
            at = slice(b * BLK, (b + 1) * BLK)
            value = dot(kb[at, lanes[h]], vb[at, lanes[h]], TN)
            state[b, lanes[h], :] = value
            sums = sums + value
        total[lanes[h], :] = sums.astype(BF16)
    for bit in reversed(range(device_bits)):
        scatter_rows(bit, 0, total, bucket_in, bucket, bs1, br1, br2)

    loads[2].wait()
    for n in range(levels):
        scale = (BLK * BLK * 2.0 ** max(n - 1, 0)) ** -0.5
        scaled_levels[n * heads:(n + 1) * heads, :] = levels_in[n] * scale
    scaled = scaled_levels[...]
    hot = (lax.broadcasted_iota(jnp.int32, (scaled.shape[1], tokens), 0) == rows[...]).astype(BF16)
    weight = jnp.zeros((scaled.shape[0], tokens), F32)
    for _ in range(3):
        piece = scaled.astype(BF16)
        scaled = scaled - piece.astype(F32)
        weight = weight + dot(piece, hot)
    wrow[...] = weight
    padded = jnp.concatenate([weight, jnp.zeros((BLK - weight.shape[0], tokens), F32)], axis=0)
    for b in range(blocks):
        at = slice(b * BLK, (b + 1) * BLK)
        wcol[at, :] = padded[:, at].T

    for m in range(local_bits):
        for b in range(blocks):
            if b >> m & 1:
                first = ((b >> m) ^ 1) << m
                value = state[first]
                for n in range(first + 1, first + (1 << m)):
                    value = value + state[n]
                local_bucket[b, m] = value.astype(BF16)
            else:
                local_bucket[b, m] = jnp.zeros((width, BLK), BF16)

    loads[3].wait()
    row_id = lax.broadcasted_iota(jnp.int32, (BLK, BLK), 0)
    col_id = lax.broadcasted_iota(jnp.int32, (BLK, BLK), 1)
    forward_near(0)
    for h in range(heads):
        for b in range(blocks):
            at = slice(b * BLK, (b + 1) * BLK)
            value = dot(kb[at, lanes[h]], qb[at, lanes[h]], NT)
            value = value * jnp.where(col_id >= row_id, wrow[h:h + 1, at], 0.0)
            score[b, lanes[h], :] = value.astype(BF16)
    forward_near(1)
    for bit in reversed(range(device_bits)):
        sum_rows(bit, 0, bucket_in, bucket_sum, bucket, br1, bs2, br2)
    for h in range(heads):
        for b in range(blocks):
            at = slice(b * BLK, (b + 1) * BLK)
            turned = qb[at, lanes[h]].astype(F32).T
            for n in range(1, levels):
                value = turned * wrow[n * heads + h:n * heads + h + 1, at]
                wq[h, (n - 1) * BLK:n * BLK, at] = value.astype(BF16)
    forward_near(2)
    loads[4].wait()
    pair = blocks // 2
    project_near(0, pair)
    for b in range(3, blocks):
        forward_near(b)
    forward_far(0)
    project_near(pair, blocks - pair)

    early = slice(0, pair * BLK)
    late = slice(pair * BLK, tokens)
    for b in range(1, blocks):
        forward_far(b)
        project_far(b - 1)
        if b == pair:
            for h in range(heads):
                for bit in range(device_bits):
                    n = local_bits + bit
                    part_early[bit, lanes[h], :] = dot(wq[h, n * BLK:(n + 1) * BLK, early], gb[early, lanes[h]])
    project_far(blocks - 1)

    for bit in reversed(range(device_bits)):
        n = local_bits + bit
        for h in range(heads):
            value = part_early[bit, lanes[h], :] + dot(wq[h, n * BLK:(n + 1) * BLK, late], gb[late, lanes[h]])
            part[bit, lanes[h], :] = value.astype(BF16)
        scatter_rows(bit, 1, part.at[bit], part_in, carried, as1, ar1, ar2)

    for h in range(heads):
        sums = [jnp.zeros((BLK, BLK), F32) for _ in range(blocks)]
        for m in range(local_bits):
            for u in range(1, blocks >> m, 2):
                at = slice(u << m << 7, (u + 1) << m << 7)
                value = dot(wq[h, m * BLK:(m + 1) * BLK, at], gb[at, lanes[h]])
                for j in range((u - 1) << m, u << m):
                    sums[j] = sums[j] + value
        for j in range(blocks):
            local_adjoint[j, lanes[h], :] = sums[j]

    def inner(b, _):
        at = pl.ds(pl.multiple_of(b * BLK, BLK), BLK)
        for h in range(heads):
            grad, key = gb[at, lanes[h]], kb[at, lanes[h]]
            value = dot(grad, vb[at, lanes[h]], NT)
            value = jnp.where(row_id >= col_id, value * wcol[at, h:h + 1], 0.0)
            intra = value.astype(BF16)
            kg[at, lanes[h]] = dot(intra, qb[at, lanes[h]], TN)
            vg[at, lanes[h]] = dot(score[b, lanes[h], :], grad)
            value = dot(intra, key)
            for m in range(local_bits):
                n = (1 + m) * heads + h
                value = value + wcol[at, n:n + 1] * dot(grad, local_bucket[b, m, lanes[h], :], NT)
            qg[at, lanes[h]] = value
        return 0

    lax.fori_loop(0, blocks, inner, 0)
    for bit in reversed(range(device_bits)):
        sum_rows(bit, 1, part_in, part_sum, carried, ar1, as2, ar2)
    for bit in range(device_bits):
        wait_result(bit, 0, bucket, br2)

    def outer(b, _):
        at = pl.ds(pl.multiple_of(b * BLK, BLK), BLK)
        for h in range(heads):
            grad = gb[at, lanes[h]]
            value = qg[at, lanes[h]]
            for bit in range(device_bits):
                n = (1 + local_bits + bit) * heads + h
                value = value + wcol[at, n:n + 1] * dot(grad, bucket[bit, lanes[h], :], NT)
            qg[at, lanes[h]] = value
        return 0

    lax.fori_loop(0, blocks, outer, 0)

    for bit in range(device_bits):
        wait_result(bit, 1, carried, ar2)
    for bit in range(device_bits):
        drain(bit, 0, total, bucket_in, bs1, bs2)
        drain(bit, 1, part.at[bit], part_in, as1, as2)
    for n in range(3):
        pltpu.make_async_copy(y, y, own_sem.at[n]).wait()
    for n in range(5):
        sent = yb.at[pl.ds(0, tokens // 2 if n < 2 else tokens), pl.ds(0, feats)]
        pltpu.make_async_copy(sent, sent, send_sem.at[n]).wait()


def finish(qg, kg, vg, kb, vb, local_adjoint, carried, qg_out, kg_out, vg_out, key_sum, value_sum, sem):
    blocks, width, _ = local_adjoint.shape
    copies = []

    def copy_rows(src, dst, at, n):
        copies.append(pltpu.make_async_copy(src.at[at], dst.at[at], sem.at[n]))
        copies[-1].start()

    for b in range(blocks):
        copy_rows(qg, qg_out, pl.ds(b * BLK, BLK), b)
    lanes = [slice(h * BLK, (h + 1) * BLK) for h in range(width // BLK)]
    arrived = carried[0].astype(F32)
    for bit in range(1, carried.shape[0]):
        arrived = arrived + carried[bit].astype(F32)
    for b in range(blocks):
        at = slice(b * BLK, (b + 1) * BLK)
        for lane in lanes:
            adjoint = (local_adjoint[b, lane, :] + arrived[lane]).astype(BF16)
            key_sum[at, lane] = kg[at, lane] + dot(vb[at, lane], adjoint, NT)
            value_sum[at, lane] = vg[at, lane] + dot(kb[at, lane], adjoint)
        copy_rows(key_sum, kg_out, pl.ds(b * BLK, BLK), blocks + b)
        copy_rows(value_sum, vg_out, pl.ds(b * BLK, BLK), 2 * blocks + b)
    for copy in copies:
        copy.wait()


def shards(grad_y, w_out, queries, keys, values, level_rows, level_table):
    tokens, width = queries.shape
    feats = grad_y.shape[1]
    heads = level_table.shape[2]
    blocks = tokens // BLK
    seq_size, head_size = lax.axis_size("seq"), lax.axis_size("head")
    device_bits = seq_size.bit_length() - 1
    local_bits = blocks.bit_length() - 1
    levels = 1 + local_bits + device_bits
    hbm = pl.BlockSpec(memory_space=pl.ANY)
    vmem = pl.BlockSpec(memory_space=pltpu.VMEM)
    dma = pltpu.SemaphoreType.DMA
    tree = pltpu.VMEM((device_bits, width // 2, BLK), BF16), pltpu.VMEM((device_bits, width // 4, BLK), BF16)
    table = level_table.transpose(1, 2, 0)
    results = pl.pallas_call(
        functools.partial(layer, seq_size, head_size, heads),
        out_shape=(
            *(pltpu.VMEM((tokens, width), F32),) * 3,
            *(pltpu.VMEM((tokens, width), BF16),) * 2,
            pltpu.VMEM((blocks, width, BLK), F32),
            pltpu.VMEM((device_bits, width, BLK), BF16),
        ),
        in_specs=[pl.BlockSpec(memory_space=pltpu.HBM)] * 5 + [vmem, pl.BlockSpec(memory_space=pltpu.HBM)],
        out_specs=(vmem,) * 7,
        scratch_shapes=[
            pltpu.VMEM((tokens, head_size * feats), BF16),
            pltpu.VMEM(w_out.shape, BF16),
            pltpu.VMEM((tokens, width), BF16),
            pltpu.VMEM((tokens, width), BF16),
            pltpu.VMEM((tokens, width), F32),
            pltpu.VMEM(table.shape, F32),
            pltpu.VMEM((levels * heads, table.shape[2]), F32),
            pltpu.VMEM((heads * levels, tokens), F32),
            pltpu.VMEM((tokens, BLK), F32),
            pltpu.VMEM((heads, (levels - 1) * BLK, tokens), BF16),
            pltpu.VMEM((blocks, width, BLK), BF16),
            pltpu.VMEM((blocks, width, BLK), F32),
            pltpu.VMEM((blocks, local_bits, width, BLK), BF16),
            pltpu.VMEM((width, BLK), BF16),
            *tree,
            pltpu.VMEM((device_bits, width, BLK), BF16),
            pltpu.VMEM((device_bits, width, BLK), BF16),
            pltpu.VMEM((device_bits, width, BLK), F32),
            *tree,
            dma((5,)),
            dma((3,)),
            dma((5,)),
            dma((head_size, blocks)),
            *[dma((device_bits,))] * 8,
        ],
        compiler_params=pltpu.CompilerParams(
            collective_id=0, has_side_effects=True, vmem_limit_bytes=54 * 2**20
        ),
        name="layer",
    )(grad_y, w_out, queries, keys, values, level_rows.reshape(1, tokens), table)

    return pl.pallas_call(
        finish,
        out_shape=(jax.ShapeDtypeStruct((tokens, width), F32),) * 3,
        in_specs=[vmem] * 7,
        out_specs=(hbm,) * 3,
        scratch_shapes=[pltpu.VMEM((tokens, width), F32)] * 2 + [dma((3 * blocks,))],
        compiler_params=pltpu.CompilerParams(vmem_limit_bytes=10 * 2**20),
        name="store",
    )(*[pltpu.with_memory_space_constraint(result, pltpu.VMEM) for result in results])


def solution(mesh):
    return jax.shard_map(
        shards,
        mesh=mesh,
        in_specs=(
            P("seq", "head"),
            P("head", None),
            P("seq", "head"),
            P("seq", "head"),
            P("seq", "head"),
            P("seq"),
            P(None, None, "head"),
        ),
        out_specs=(P("seq", "head"), P("seq", "head"), P("seq", "head")),
        check_vma=False,
    )
```

```python
import functools

import jax
import jax.numpy as jnp
from jax import lax
from jax.experimental import pallas as pl
from jax.experimental.pallas import tpu as pltpu
from jax.sharding import PartitionSpec as P

BLK = 128
CORES = 2
MESH = pl.DeviceIdType.MESH
NN = (((1,), (0,)), ((), ()))
NT = (((1,), (1,)), ((), ()))
TN = (((0,), (0,)), ((), ()))
F32 = jnp.float32
BF16 = jnp.bfloat16


def dot(a, b, dims=NN):
    return lax.dot_general(a, b, dims, preferred_element_type=F32)


def layer(
    seq_size, head_size, heads,
    y, w, q, k, v, rows, table,
    qg, kg, vg, kb, vb, local_adjoint, carried,
    yb, wb, qb, gb, near, levels_in, scaled_levels,
    wrow, wcol, wq, score, state, local_bucket,
    total, bucket_in, bucket_sum, bucket,
    part, part_early, part_in, part_sum,
    load_sem, own_sem, send_sem, y_sem,
    bs1, br1, bs2, br2, as1, ar1, as2, ar2
):
    tokens, feats = y.shape
    width = heads * BLK
    blocks = tokens // BLK
    local_bits = blocks.bit_length() - 1
    device_bits = seq_size.bit_length() - 1
    levels = 1 + local_bits + device_bits
    ring = head_size // CORES
    pos = lax.axis_index("seq")
    head = lax.axis_index("head")
    x, core = head // CORES, lax.rem(head, CORES)
    right = lax.rem(x + 1, ring) * CORES + core
    left = lax.rem(x + ring - 1, ring) * CORES + core
    across = lax.rem(x + 2, ring) * CORES + core
    near_chips, far_chip = (x, lax.rem(x + 1, ring), lax.rem(x + ring - 1, ring)), lax.rem(x + 2, ring)
    twin = x * CORES + 1 - core

    loads = [
        pltpu.make_async_copy(src, dst, load_sem.at[n])
        for n, (src, dst) in enumerate(((k, kb), (v, vb), (table, levels_in), (q, qb), (w, wb)))
    ]
    for load in loads:
        load.start()

    barrier = pltpu.get_barrier_semaphore()

    def greet(step, _):
        peer = lax.rem(pos + step, seq_size)
        pl.semaphore_signal(barrier, inc=1, device_id=(peer, head), device_id_type=MESH)
        return 0

    for peer in (right, left, twin):
        pl.semaphore_signal(barrier, inc=1, device_id=(pos, peer), device_id_type=MESH)
    lax.fori_loop(1, seq_size, greet, 0, unroll=True)
    pl.semaphore_wait(barrier, seq_size - 1 + 3)

    def columns(owner):
        return pl.ds(pl.multiple_of(owner * feats, feats), feats)

    def place(owner, row, count):
        return yb.at[pl.ds(row, count), columns(owner)]

    def send(src, dst, sem_out, sem_in, peer):
        pltpu.make_async_remote_copy(
            src_ref=src, dst_ref=dst, send_sem=sem_out, recv_sem=sem_in,
            device_id=peer, device_id_type=MESH,
        ).start()

    for b in range(blocks):
        src = y.at[pl.ds(b * BLK, BLK), :]
        for n, peer in enumerate((right, left, twin)):
            send(src, place(head, b * BLK, BLK), own_sem.at[n], y_sem.at[head, b], (pos, peer))
        pltpu.make_async_copy(src, place(head, b * BLK, BLK), y_sem.at[head, b]).start()

    def wait_y(owner, b):
        here = place(owner, b * BLK, BLK)
        pltpu.make_async_copy(here, here, y_sem.at[owner, b]).wait()

    for bit in range(device_bits):
        has = lax.rem(pos // (1 << bit), 2)

        @pl.when(has == 0)
        def _():
            bucket[bit] = jnp.zeros((width, BLK), BF16)

        @pl.when(has == 1)
        def _():
            carried[bit] = jnp.zeros((width, BLK), BF16)

    half = BLK // 2

    def forward_near(b):
        wait_y(left, b)
        piece = place(left, b * BLK, half)
        send(piece, piece, send_sem.at[0], y_sem.at[left, b], (pos, right))
        piece = place(left, b * BLK, BLK)
        send(piece, piece, send_sem.at[2], y_sem.at[left, b], (pos, twin))
        wait_y(right, b)
        piece = place(right, b * BLK + half, half)
        send(piece, piece, send_sem.at[1], y_sem.at[right, b], (pos, left))
        piece = place(right, b * BLK, BLK)
        send(piece, piece, send_sem.at[3], y_sem.at[right, b], (pos, twin))

    def forward_far(b):
        wait_y(across, b)
        piece = place(across, b * BLK, BLK)
        send(piece, piece, send_sem.at[4], y_sem.at[across, b], (pos, twin))

    def take_twin(owners, b):
        for owner in owners:
            wait_y(owner + 1 - 2 * core, b)

    def product(at, chip):
        inner = pl.ds(pl.multiple_of(chip * CORES * feats, CORES * feats), CORES * feats)
        return dot(yb[at, inner], wb[:, inner], NT)

    def project_near(b, count):
        for n in range(b, b + count):
            wait_y(head, n)
            take_twin((head, left, right), n)
        at = pl.ds(b * BLK, count * BLK)
        value = product(at, near_chips[0])
        for chip in near_chips[1:]:
            value = value + product(at, chip)
        near[at, :] = value

    def project_far(b):
        take_twin((across,), b)
        at = pl.ds(b * BLK, BLK)
        gb[at, :] = (near[at, :] + product(at, far_chip)).astype(BF16)

    def spans(bit):
        count = 2 << bit
        return count, width // count, lax.rem(pos, count)

    def scatter_rows(bit, src_bit, data, landing, result, sem_out, sem_in, sem_result):
        count, size, index = spans(bit)

        @pl.when(lax.rem(pos // (1 << bit), 2) == src_bit)
        def _():
            if bit == 0:
                send(data, result.at[0], sem_out.at[0], sem_result.at[0], (pos + 1 - 2 * src_bit, head))
                return
            slot = landing.at[bit, pl.ds(pl.multiple_of(lax.rem(index, 1 << bit) * size, size), size), :]

            def step(off, _):
                owner = lax.rem(index + off, count)
                src = data.at[pl.ds(pl.multiple_of(owner * size, size), size), :]
                send(src, slot, sem_out.at[bit], sem_in.at[bit], (pos - index + owner, head))
                return 0

            lax.fori_loop(1, count, step, 0)
            src = data.at[pl.ds(pl.multiple_of(index * size, size), size), :]
            pltpu.make_async_copy(src, slot, sem_in.at[bit]).start()

    def sum_rows(bit, src_bit, landing, summed, result, sem_in, sem_out, sem_result):
        if bit == 0:
            return
        count, size, index = spans(bit)
        here = landing.at[bit]
        pltpu.make_async_copy(here, here, sem_in.at[bit]).wait()
        value = landing[bit, 0:size, :].astype(F32)
        for n in range(1, 1 << bit):
            value = value + landing[bit, n * size:(n + 1) * size, :].astype(F32)
        summed[bit, 0:size, :] = value.astype(BF16)
        src = summed.at[bit, pl.ds(0, size), :]
        dst = result.at[bit, pl.ds(pl.multiple_of(index * size, size), size), :]
        first = (1 - src_bit) * (1 << bit)
        own = lax.rem(index, 1 << bit)
        sink = lax.rem(pos // (1 << bit), 2) != src_bit

        def step(off, _):
            peer = first + lax.rem(own + off, 1 << bit)
            send(src, dst, sem_out.at[bit], sem_result.at[bit], (pos - index + peer, head))
            return 0

        lax.fori_loop(1, 1 << bit, step, 0)

        @pl.when(sink)
        def _():
            pltpu.make_async_copy(src, dst, sem_result.at[bit]).start()

        @pl.when(jnp.logical_not(sink))
        def _():
            step(0, 0)

    def wait_result(bit, src_bit, result, sem_result):
        @pl.when(lax.rem(pos // (1 << bit), 2) != src_bit)
        def _():
            here = result.at[bit]
            pltpu.make_async_copy(here, here, sem_result.at[bit]).wait()

    def drain(bit, src_bit, data, landing, sem_first, sem_second):
        count, size, _ = spans(bit)
        source = lax.rem(pos // (1 << bit), 2) == src_bit

        @pl.when(source)
        def _():
            sent = data if bit == 0 else data.at[pl.ds(0, width - size), :]
            pltpu.make_async_copy(sent, sent, sem_first.at[bit]).wait()
            if bit > 0:
                again = landing.at[bit]
                pltpu.make_async_copy(again, again, sem_second.at[bit]).wait()

        if bit > 0:
            @pl.when(jnp.logical_not(source))
            def _():
                again = landing.at[bit, pl.ds(0, width // 2 - size), :]
                pltpu.make_async_copy(again, again, sem_second.at[bit]).wait()

    loads[0].wait()
    loads[1].wait()
    lanes = [slice(h * BLK, (h + 1) * BLK) for h in range(heads)]
    for h in range(heads):
        sums = jnp.zeros((BLK, BLK), F32)
        for b in range(blocks):
            at = slice(b * BLK, (b + 1) * BLK)
            value = dot(kb[at, lanes[h]], vb[at, lanes[h]], TN)
            state[b, lanes[h], :] = value
            sums = sums + value
        total[lanes[h], :] = sums.astype(BF16)
    for bit in reversed(range(device_bits)):
        scatter_rows(bit, 0, total, bucket_in, bucket, bs1, br1, br2)

    loads[2].wait()
    for n in range(levels):
        scale = (BLK * BLK * 2.0 ** max(n - 1, 0)) ** -0.5
        scaled_levels[n * heads:(n + 1) * heads, :] = levels_in[n] * scale
    scaled = scaled_levels[...]
    hot = (lax.broadcasted_iota(jnp.int32, (scaled.shape[1], tokens), 0) == rows[...]).astype(BF16)
    weight = jnp.zeros((scaled.shape[0], tokens), F32)
    for _ in range(3):
        piece = scaled.astype(BF16)
        scaled = scaled - piece.astype(F32)
        weight = weight + dot(piece, hot)
    wrow[...] = weight
    padded = jnp.concatenate([weight, jnp.zeros((BLK - weight.shape[0], tokens), F32)], axis=0)
    for b in range(blocks):
        at = slice(b * BLK, (b + 1) * BLK)
        wcol[at, :] = padded[:, at].T

    for m in range(local_bits):
        for b in range(blocks):
            if b >> m & 1:
                first = ((b >> m) ^ 1) << m
                value = state[first]
                for n in range(first + 1, first + (1 << m)):
                    value = value + state[n]
                local_bucket[b, m] = value.astype(BF16)
            else:
                local_bucket[b, m] = jnp.zeros((width, BLK), BF16)

    loads[3].wait()
    row_id = lax.broadcasted_iota(jnp.int32, (BLK, BLK), 0)
    col_id = lax.broadcasted_iota(jnp.int32, (BLK, BLK), 1)
    forward_near(0)
    for h in range(heads):
        for b in range(blocks):
            at = slice(b * BLK, (b + 1) * BLK)
            value = dot(kb[at, lanes[h]], qb[at, lanes[h]], NT)
            value = value * jnp.where(col_id >= row_id, wrow[h:h + 1, at], 0.0)
            score[b, lanes[h], :] = value.astype(BF16)
    forward_near(1)
    for h in range(heads):
        for b in range(blocks):
            at = slice(b * BLK, (b + 1) * BLK)
            turned = qb[at, lanes[h]].astype(F32).T
            for n in range(1, levels):
                value = turned * wrow[n * heads + h:n * heads + h + 1, at]
                wq[h, (n - 1) * BLK:n * BLK, at] = value.astype(BF16)
    for b in range(2, blocks):
        forward_near(b)
    for bit in reversed(range(device_bits)):
        sum_rows(bit, 0, bucket_in, bucket_sum, bucket, br1, bs2, br2)
    loads[4].wait()
    pair = blocks // 2
    project_near(0, pair)
    project_near(pair, blocks - pair)
    forward_far(0)

    early = slice(0, pair * BLK)
    late = slice(pair * BLK, tokens)
    for b in range(1, blocks):
        forward_far(b)
    for b in range(1, blocks):
        project_far(b - 1)
        if b == pair:
            for h in range(heads):
                for bit in range(device_bits):
                    n = local_bits + bit
                    part_early[bit, lanes[h], :] = dot(wq[h, n * BLK:(n + 1) * BLK, early], gb[early, lanes[h]])
    project_far(blocks - 1)

    for bit in reversed(range(device_bits)):
        n = local_bits + bit
        for h in range(heads):
            value = part_early[bit, lanes[h], :] + dot(wq[h, n * BLK:(n + 1) * BLK, late], gb[late, lanes[h]])
            part[bit, lanes[h], :] = value.astype(BF16)
        scatter_rows(bit, 1, part.at[bit], part_in, carried, as1, ar1, ar2)

    for h in range(heads):
        sums = [jnp.zeros((BLK, BLK), F32) for _ in range(blocks)]
        for m in range(local_bits):
            for u in range(1, blocks >> m, 2):
                at = slice(u << m << 7, (u + 1) << m << 7)
                value = dot(wq[h, m * BLK:(m + 1) * BLK, at], gb[at, lanes[h]])
                for j in range((u - 1) << m, u << m):
                    sums[j] = sums[j] + value
        for j in range(blocks):
            local_adjoint[j, lanes[h], :] = sums[j]

    def inner(b, _):
        at = pl.ds(pl.multiple_of(b * BLK, BLK), BLK)
        for h in range(heads):
            grad, key = gb[at, lanes[h]], kb[at, lanes[h]]
            value = dot(grad, vb[at, lanes[h]], NT)
            value = jnp.where(row_id >= col_id, value * wcol[at, h:h + 1], 0.0)
            intra = value.astype(BF16)
            kg[at, lanes[h]] = dot(intra, qb[at, lanes[h]], TN)
            vg[at, lanes[h]] = dot(score[b, lanes[h], :], grad)
            value = dot(intra, key)
            for m in range(local_bits):
                n = (1 + m) * heads + h
                value = value + wcol[at, n:n + 1] * dot(grad, local_bucket[b, m, lanes[h], :], NT)
            qg[at, lanes[h]] = value
        return 0

    lax.fori_loop(0, blocks, inner, 0)
    for bit in reversed(range(device_bits)):
        sum_rows(bit, 1, part_in, part_sum, carried, ar1, as2, ar2)
    for bit in range(device_bits):
        wait_result(bit, 0, bucket, br2)

    def outer(b, _):
        at = pl.ds(pl.multiple_of(b * BLK, BLK), BLK)
        for h in range(heads):
            grad = gb[at, lanes[h]]
            value = qg[at, lanes[h]]
            for bit in range(device_bits):
                n = (1 + local_bits + bit) * heads + h
                value = value + wcol[at, n:n + 1] * dot(grad, bucket[bit, lanes[h], :], NT)
            qg[at, lanes[h]] = value
        return 0

    lax.fori_loop(0, blocks, outer, 0)

    for bit in range(device_bits):
        wait_result(bit, 1, carried, ar2)
    for bit in range(device_bits):
        drain(bit, 0, total, bucket_in, bs1, bs2)
        drain(bit, 1, part.at[bit], part_in, as1, as2)
    for n in range(3):
        pltpu.make_async_copy(y, y, own_sem.at[n]).wait()
    for n in range(5):
        sent = yb.at[pl.ds(0, tokens // 2 if n < 2 else tokens), pl.ds(0, feats)]
        pltpu.make_async_copy(sent, sent, send_sem.at[n]).wait()


def finish(qg, kg, vg, kb, vb, local_adjoint, carried, qg_out, kg_out, vg_out, key_sum, value_sum, sem):
    blocks, width, _ = local_adjoint.shape
    copies = []

    def copy_rows(src, dst, at, n):
        copies.append(pltpu.make_async_copy(src.at[at], dst.at[at], sem.at[n]))
        copies[-1].start()

    for b in range(blocks):
        copy_rows(qg, qg_out, pl.ds(b * BLK, BLK), b)
    lanes = [slice(h * BLK, (h + 1) * BLK) for h in range(width // BLK)]
    arrived = carried[0].astype(F32)
    for bit in range(1, carried.shape[0]):
        arrived = arrived + carried[bit].astype(F32)
    for b in range(blocks):
        at = slice(b * BLK, (b + 1) * BLK)
        for lane in lanes:
            adjoint = (local_adjoint[b, lane, :] + arrived[lane]).astype(BF16)
            key_sum[at, lane] = kg[at, lane] + dot(vb[at, lane], adjoint, NT)
            value_sum[at, lane] = vg[at, lane] + dot(kb[at, lane], adjoint)
        copy_rows(key_sum, kg_out, pl.ds(b * BLK, BLK), blocks + b)
        copy_rows(value_sum, vg_out, pl.ds(b * BLK, BLK), 2 * blocks + b)
    for copy in copies:
        copy.wait()


def shards(grad_y, w_out, queries, keys, values, level_rows, level_table):
    tokens, width = queries.shape
    feats = grad_y.shape[1]
    heads = level_table.shape[2]
    blocks = tokens // BLK
    seq_size, head_size = lax.axis_size("seq"), lax.axis_size("head")
    device_bits = seq_size.bit_length() - 1
    local_bits = blocks.bit_length() - 1
    levels = 1 + local_bits + device_bits
    hbm = pl.BlockSpec(memory_space=pl.ANY)
    vmem = pl.BlockSpec(memory_space=pltpu.VMEM)
    dma = pltpu.SemaphoreType.DMA
    tree = pltpu.VMEM((device_bits, width // 2, BLK), BF16), pltpu.VMEM((device_bits, width // 4, BLK), BF16)
    table = level_table.transpose(1, 2, 0)
    results = pl.pallas_call(
        functools.partial(layer, seq_size, head_size, heads),
        out_shape=(
            *(pltpu.VMEM((tokens, width), F32),) * 3,
            *(pltpu.VMEM((tokens, width), BF16),) * 2,
            pltpu.VMEM((blocks, width, BLK), F32),
            pltpu.VMEM((device_bits, width, BLK), BF16),
        ),
        in_specs=[pl.BlockSpec(memory_space=pltpu.HBM)] * 5 + [vmem, pl.BlockSpec(memory_space=pltpu.HBM)],
        out_specs=(vmem,) * 7,
        scratch_shapes=[
            pltpu.VMEM((tokens, head_size * feats), BF16),
            pltpu.VMEM(w_out.shape, BF16),
            pltpu.VMEM((tokens, width), BF16),
            pltpu.VMEM((tokens, width), BF16),
            pltpu.VMEM((tokens, width), F32),
            pltpu.VMEM(table.shape, F32),
            pltpu.VMEM((levels * heads, table.shape[2]), F32),
            pltpu.VMEM((heads * levels, tokens), F32),
            pltpu.VMEM((tokens, BLK), F32),
            pltpu.VMEM((heads, (levels - 1) * BLK, tokens), BF16),
            pltpu.VMEM((blocks, width, BLK), BF16),
            pltpu.VMEM((blocks, width, BLK), F32),
            pltpu.VMEM((blocks, local_bits, width, BLK), BF16),
            pltpu.VMEM((width, BLK), BF16),
            *tree,
            pltpu.VMEM((device_bits, width, BLK), BF16),
            pltpu.VMEM((device_bits, width, BLK), BF16),
            pltpu.VMEM((device_bits, width, BLK), F32),
            *tree,
            dma((5,)),
            dma((3,)),
            dma((5,)),
            dma((head_size, blocks)),
            *[dma((device_bits,))] * 8,
        ],
        compiler_params=pltpu.CompilerParams(
            collective_id=0, has_side_effects=True, vmem_limit_bytes=54 * 2**20
        ),
        name="layer",
    )(grad_y, w_out, queries, keys, values, level_rows.reshape(1, tokens), table)

    return pl.pallas_call(
        finish,
        out_shape=(jax.ShapeDtypeStruct((tokens, width), F32),) * 3,
        in_specs=[vmem] * 7,
        out_specs=(hbm,) * 3,
        scratch_shapes=[pltpu.VMEM((tokens, width), F32)] * 2 + [dma((3 * blocks,))],
        compiler_params=pltpu.CompilerParams(vmem_limit_bytes=10 * 2**20),
        name="store",
    )(*[pltpu.with_memory_space_constraint(result, pltpu.VMEM) for result in results])


def solution(mesh):
    return jax.shard_map(
        shards,
        mesh=mesh,
        in_specs=(
            P("seq", "head"),
            P("head", None),
            P("seq", "head"),
            P("seq", "head"),
            P("seq", "head"),
            P("seq"),
            P(None, None, "head"),
        ),
        out_specs=(P("seq", "head"), P("seq", "head"), P("seq", "head")),
        check_vma=False,
    )
```

```python
import functools

import jax
import jax.numpy as jnp
from jax import lax
from jax.experimental import pallas as pl
from jax.experimental.pallas import tpu as pltpu
from jax.sharding import PartitionSpec as P

BLK = 128
CORES = 2
MESH = pl.DeviceIdType.MESH
NN = (((1,), (0,)), ((), ()))
NT = (((1,), (1,)), ((), ()))
TN = (((0,), (0,)), ((), ()))
F32 = jnp.float32
BF16 = jnp.bfloat16


def dot(a, b, dims=NN):
    return lax.dot_general(a, b, dims, preferred_element_type=F32)


def layer(
    seq_size, head_size, heads,
    y, w, q, k, v, rows, table,
    qg, kg, vg, kb, vb, local_adjoint, carried,
    yb, wb, qb, gb, near, levels_in, scaled_levels,
    wrow, wcol, wq, score, state, local_bucket,
    total, bucket_in, bucket_sum, bucket,
    part, part_early, part_in, part_sum,
    load_sem, own_sem, send_sem, y_sem,
    bs1, br1, bs2, br2, as1, ar1, as2, ar2
):
    tokens, feats = y.shape
    width = heads * BLK
    blocks = tokens // BLK
    local_bits = blocks.bit_length() - 1
    device_bits = seq_size.bit_length() - 1
    levels = 1 + local_bits + device_bits
    ring = head_size // CORES
    pos = lax.axis_index("seq")
    head = lax.axis_index("head")
    x, core = head // CORES, lax.rem(head, CORES)
    right = lax.rem(x + 1, ring) * CORES + core
    left = lax.rem(x + ring - 1, ring) * CORES + core
    across = lax.rem(x + 2, ring) * CORES + core
    near_chips, far_chip = (x, lax.rem(x + 1, ring), lax.rem(x + ring - 1, ring)), lax.rem(x + 2, ring)
    twin = x * CORES + 1 - core

    loads = [
        pltpu.make_async_copy(src, dst, load_sem.at[n])
        for n, (src, dst) in enumerate(((k, kb), (v, vb), (table, levels_in), (q, qb), (w, wb)))
    ]
    for load in loads:
        load.start()

    barrier = pltpu.get_barrier_semaphore()

    def greet(step, _):
        peer = lax.rem(pos + step, seq_size)
        pl.semaphore_signal(barrier, inc=1, device_id=(peer, head), device_id_type=MESH)
        return 0

    for peer in (right, left, twin):
        pl.semaphore_signal(barrier, inc=1, device_id=(pos, peer), device_id_type=MESH)
    lax.fori_loop(1, seq_size, greet, 0, unroll=True)
    pl.semaphore_wait(barrier, seq_size - 1 + 3)

    def columns(owner):
        return pl.ds(pl.multiple_of(owner * feats, feats), feats)

    def place(owner, row, count):
        return yb.at[pl.ds(row, count), columns(owner)]

    def send(src, dst, sem_out, sem_in, peer):
        pltpu.make_async_remote_copy(
            src_ref=src, dst_ref=dst, send_sem=sem_out, recv_sem=sem_in,
            device_id=peer, device_id_type=MESH,
        ).start()

    for b in range(blocks):
        src = y.at[pl.ds(b * BLK, BLK), :]
        for n, peer in enumerate((right, left, twin)):
            send(src, place(head, b * BLK, BLK), own_sem.at[n], y_sem.at[head, b], (pos, peer))
        pltpu.make_async_copy(src, place(head, b * BLK, BLK), y_sem.at[head, b]).start()

    def wait_y(owner, b):
        here = place(owner, b * BLK, BLK)
        pltpu.make_async_copy(here, here, y_sem.at[owner, b]).wait()

    for bit in range(device_bits):
        has = lax.rem(pos // (1 << bit), 2)

        @pl.when(has == 0)
        def _():
            bucket[bit] = jnp.zeros((width, BLK), BF16)

        @pl.when(has == 1)
        def _():
            carried[bit] = jnp.zeros((width, BLK), BF16)

    half = BLK // 2

    def forward_near(b):
        wait_y(left, b)
        piece = place(left, b * BLK, half)
        send(piece, piece, send_sem.at[0], y_sem.at[left, b], (pos, right))
        piece = place(left, b * BLK, BLK)
        send(piece, piece, send_sem.at[2], y_sem.at[left, b], (pos, twin))
        wait_y(right, b)
        piece = place(right, b * BLK + half, half)
        send(piece, piece, send_sem.at[1], y_sem.at[right, b], (pos, left))
        piece = place(right, b * BLK, BLK)
        send(piece, piece, send_sem.at[3], y_sem.at[right, b], (pos, twin))

    def forward_far(b):
        wait_y(across, b)
        piece = place(across, b * BLK, BLK)
        send(piece, piece, send_sem.at[4], y_sem.at[across, b], (pos, twin))

    def take_twin(owners, b):
        for owner in owners:
            wait_y(owner + 1 - 2 * core, b)

    def product(at, chip):
        inner = pl.ds(pl.multiple_of(chip * CORES * feats, CORES * feats), CORES * feats)
        return dot(yb[at, inner], wb[:, inner], NT)

    def project_near(b, count):
        for n in range(b, b + count):
            wait_y(head, n)
            take_twin((head, left, right), n)
        at = pl.ds(b * BLK, count * BLK)
        value = product(at, near_chips[0])
        for chip in near_chips[1:]:
            value = value + product(at, chip)
        near[at, :] = value

    def project_far(b):
        take_twin((across,), b)
        at = pl.ds(b * BLK, BLK)
        gb[at, :] = (near[at, :] + product(at, far_chip)).astype(BF16)

    def spans(bit):
        count = 2 << bit
        return count, width // count, lax.rem(pos, count)

    def scatter_rows(bit, src_bit, data, landing, result, sem_out, sem_in, sem_result):
        count, size, index = spans(bit)

        @pl.when(lax.rem(pos // (1 << bit), 2) == src_bit)
        def _():
            if bit == 0:
                send(data, result.at[0], sem_out.at[0], sem_result.at[0], (pos + 1 - 2 * src_bit, head))
                return
            slot = landing.at[bit, pl.ds(pl.multiple_of(lax.rem(index, 1 << bit) * size, size), size), :]

            def step(off, _):
                owner = lax.rem(index + off, count)
                src = data.at[pl.ds(pl.multiple_of(owner * size, size), size), :]
                send(src, slot, sem_out.at[bit], sem_in.at[bit], (pos - index + owner, head))
                return 0

            lax.fori_loop(1, count, step, 0)
            src = data.at[pl.ds(pl.multiple_of(index * size, size), size), :]
            pltpu.make_async_copy(src, slot, sem_in.at[bit]).start()

    def sum_rows(bit, src_bit, landing, summed, result, sem_in, sem_out, sem_result):
        if bit == 0:
            return
        count, size, index = spans(bit)
        here = landing.at[bit]
        pltpu.make_async_copy(here, here, sem_in.at[bit]).wait()
        value = landing[bit, 0:size, :].astype(F32)
        for n in range(1, 1 << bit):
            value = value + landing[bit, n * size:(n + 1) * size, :].astype(F32)
        summed[bit, 0:size, :] = value.astype(BF16)
        src = summed.at[bit, pl.ds(0, size), :]
        dst = result.at[bit, pl.ds(pl.multiple_of(index * size, size), size), :]
        first = (1 - src_bit) * (1 << bit)
        own = lax.rem(index, 1 << bit)
        sink = lax.rem(pos // (1 << bit), 2) != src_bit

        def step(off, _):
            peer = first + lax.rem(own + off, 1 << bit)
            send(src, dst, sem_out.at[bit], sem_result.at[bit], (pos - index + peer, head))
            return 0

        lax.fori_loop(1, 1 << bit, step, 0)

        @pl.when(sink)
        def _():
            pltpu.make_async_copy(src, dst, sem_result.at[bit]).start()

        @pl.when(jnp.logical_not(sink))
        def _():
            step(0, 0)

    def wait_result(bit, src_bit, result, sem_result):
        @pl.when(lax.rem(pos // (1 << bit), 2) != src_bit)
        def _():
            here = result.at[bit]
            pltpu.make_async_copy(here, here, sem_result.at[bit]).wait()

    def drain(bit, src_bit, data, landing, sem_first, sem_second):
        count, size, _ = spans(bit)
        source = lax.rem(pos // (1 << bit), 2) == src_bit

        @pl.when(source)
        def _():
            sent = data if bit == 0 else data.at[pl.ds(0, width - size), :]
            pltpu.make_async_copy(sent, sent, sem_first.at[bit]).wait()
            if bit > 0:
                again = landing.at[bit]
                pltpu.make_async_copy(again, again, sem_second.at[bit]).wait()

        if bit > 0:
            @pl.when(jnp.logical_not(source))
            def _():
                again = landing.at[bit, pl.ds(0, width // 2 - size), :]
                pltpu.make_async_copy(again, again, sem_second.at[bit]).wait()

    loads[0].wait()
    loads[1].wait()
    lanes = [slice(h * BLK, (h + 1) * BLK) for h in range(heads)]
    for h in range(heads):
        sums = jnp.zeros((BLK, BLK), F32)
        for b in range(blocks):
            at = slice(b * BLK, (b + 1) * BLK)
            value = dot(kb[at, lanes[h]], vb[at, lanes[h]], TN)
            state[b, lanes[h], :] = value
            sums = sums + value
        total[lanes[h], :] = sums.astype(BF16)
    for bit in reversed(range(device_bits)):
        scatter_rows(bit, 0, total, bucket_in, bucket, bs1, br1, br2)

    loads[2].wait()
    for n in range(levels):
        scale = (BLK * BLK * 2.0 ** max(n - 1, 0)) ** -0.5
        scaled_levels[n * heads:(n + 1) * heads, :] = levels_in[n] * scale
    scaled = scaled_levels[...]
    hot = (lax.broadcasted_iota(jnp.int32, (scaled.shape[1], tokens), 0) == rows[...]).astype(BF16)
    weight = jnp.zeros((scaled.shape[0], tokens), F32)
    for _ in range(3):
        piece = scaled.astype(BF16)
        scaled = scaled - piece.astype(F32)
        weight = weight + dot(piece, hot)
    wrow[...] = weight
    padded = jnp.concatenate([weight, jnp.zeros((BLK - weight.shape[0], tokens), F32)], axis=0)
    for b in range(blocks):
        at = slice(b * BLK, (b + 1) * BLK)
        wcol[at, :] = padded[:, at].T

    for m in range(local_bits):
        for b in range(blocks):
            if b >> m & 1:
                first = ((b >> m) ^ 1) << m
                value = state[first]
                for n in range(first + 1, first + (1 << m)):
                    value = value + state[n]
                local_bucket[b, m] = value.astype(BF16)
            else:
                local_bucket[b, m] = jnp.zeros((width, BLK), BF16)

    loads[3].wait()
    row_id = lax.broadcasted_iota(jnp.int32, (BLK, BLK), 0)
    col_id = lax.broadcasted_iota(jnp.int32, (BLK, BLK), 1)
    forward_near(0)
    for h in range(heads):
        for b in range(blocks):
            at = slice(b * BLK, (b + 1) * BLK)
            value = dot(kb[at, lanes[h]], qb[at, lanes[h]], NT)
            value = value * jnp.where(col_id >= row_id, wrow[h:h + 1, at], 0.0)
            score[b, lanes[h], :] = value.astype(BF16)
    forward_near(1)
    for h in range(heads):
        for b in range(blocks):
            at = slice(b * BLK, (b + 1) * BLK)
            turned = qb[at, lanes[h]].astype(F32).T
            for n in range(1, levels):
                value = turned * wrow[n * heads + h:n * heads + h + 1, at]
                wq[h, (n - 1) * BLK:n * BLK, at] = value.astype(BF16)
    for b in range(2, blocks):
        forward_near(b)
    for bit in reversed(range(device_bits)):
        sum_rows(bit, 0, bucket_in, bucket_sum, bucket, br1, bs2, br2)
    loads[4].wait()
    pair = blocks // 2
    project_near(0, pair)
    project_near(pair, blocks - pair)
    forward_far(0)

    early = slice(0, pair * BLK)
    late = slice(pair * BLK, tokens)
    for b in range(1, blocks):
        forward_far(b)
    for b in range(1, blocks):
        project_far(b - 1)
        if b == pair:
            for h in range(heads):
                for bit in range(device_bits):
                    n = local_bits + bit
                    part_early[bit, lanes[h], :] = dot(wq[h, n * BLK:(n + 1) * BLK, early], gb[early, lanes[h]])
    project_far(blocks - 1)

    for bit in reversed(range(device_bits)):
        n = local_bits + bit
        for h in range(heads):
            value = part_early[bit, lanes[h], :] + dot(wq[h, n * BLK:(n + 1) * BLK, late], gb[late, lanes[h]])
            part[bit, lanes[h], :] = value.astype(BF16)
        scatter_rows(bit, 1, part.at[bit], part_in, carried, as1, ar1, ar2)

    for h in range(heads):
        sums = [jnp.zeros((BLK, BLK), F32) for _ in range(blocks)]
        for m in range(local_bits):
            for u in range(1, blocks >> m, 2):
                at = slice(u << m << 7, (u + 1) << m << 7)
                value = dot(wq[h, m * BLK:(m + 1) * BLK, at], gb[at, lanes[h]])
                for j in range((u - 1) << m, u << m):
                    sums[j] = sums[j] + value
        for j in range(blocks):
            local_adjoint[j, lanes[h], :] = sums[j]

    def inner(b, _):
        at = pl.ds(pl.multiple_of(b * BLK, BLK), BLK)
        for h in range(heads):
            grad, key = gb[at, lanes[h]], kb[at, lanes[h]]
            value = dot(grad, vb[at, lanes[h]], NT)
            value = jnp.where(row_id >= col_id, value * wcol[at, h:h + 1], 0.0)
            intra = value.astype(BF16)
            kg[at, lanes[h]] = dot(intra, qb[at, lanes[h]], TN)
            vg[at, lanes[h]] = dot(score[b, lanes[h], :], grad)
            value = dot(intra, key)
            for m in range(local_bits):
                n = (1 + m) * heads + h
                value = value + wcol[at, n:n + 1] * dot(grad, local_bucket[b, m, lanes[h], :], NT)
            qg[at, lanes[h]] = value
        return 0

    lax.fori_loop(0, blocks, inner, 0)
    for bit in reversed(range(device_bits)):
        sum_rows(bit, 1, part_in, part_sum, carried, ar1, as2, ar2)
    for bit in range(device_bits):
        wait_result(bit, 0, bucket, br2)

    def outer(b, _):
        at = pl.ds(pl.multiple_of(b * BLK, BLK), BLK)
        for h in range(heads):
            grad = gb[at, lanes[h]]
            value = qg[at, lanes[h]]
            for bit in range(device_bits):
                n = (1 + local_bits + bit) * heads + h
                value = value + wcol[at, n:n + 1] * dot(grad, bucket[bit, lanes[h], :], NT)
            qg[at, lanes[h]] = value
        return 0

    lax.fori_loop(0, blocks, outer, 0)

    for bit in range(device_bits):
        drain(bit, 0, total, bucket_in, bs1, bs2)
        drain(bit, 1, part.at[bit], part_in, as1, as2)
    for n in range(3):
        pltpu.make_async_copy(y, y, own_sem.at[n]).wait()
    for n in range(5):
        sent = yb.at[pl.ds(0, tokens // 2 if n < 2 else tokens), pl.ds(0, feats)]
        pltpu.make_async_copy(sent, sent, send_sem.at[n]).wait()
    for bit in range(device_bits):
        wait_result(bit, 1, carried, ar2)


def finish(qg, kg, vg, kb, vb, local_adjoint, carried, qg_out, kg_out, vg_out, key_sum, value_sum, sem):
    blocks, width, _ = local_adjoint.shape
    copies = []

    def copy_rows(src, dst, at, n):
        copies.append(pltpu.make_async_copy(src.at[at], dst.at[at], sem.at[n]))
        copies[-1].start()

    for b in range(blocks):
        copy_rows(qg, qg_out, pl.ds(b * BLK, BLK), b)
    lanes = [slice(h * BLK, (h + 1) * BLK) for h in range(width // BLK)]
    arrived = carried[0].astype(F32)
    for bit in range(1, carried.shape[0]):
        arrived = arrived + carried[bit].astype(F32)
    for b in range(blocks):
        at = slice(b * BLK, (b + 1) * BLK)
        for lane in lanes:
            adjoint = (local_adjoint[b, lane, :] + arrived[lane]).astype(BF16)
            key_sum[at, lane] = kg[at, lane] + dot(vb[at, lane], adjoint, NT)
            value_sum[at, lane] = vg[at, lane] + dot(kb[at, lane], adjoint)
        copy_rows(key_sum, kg_out, pl.ds(b * BLK, BLK), blocks + b)
        copy_rows(value_sum, vg_out, pl.ds(b * BLK, BLK), 2 * blocks + b)
    for copy in copies:
        copy.wait()


def shards(grad_y, w_out, queries, keys, values, level_rows, level_table):
    tokens, width = queries.shape
    feats = grad_y.shape[1]
    heads = level_table.shape[2]
    blocks = tokens // BLK
    seq_size, head_size = lax.axis_size("seq"), lax.axis_size("head")
    device_bits = seq_size.bit_length() - 1
    local_bits = blocks.bit_length() - 1
    levels = 1 + local_bits + device_bits
    hbm = pl.BlockSpec(memory_space=pl.ANY)
    vmem = pl.BlockSpec(memory_space=pltpu.VMEM)
    dma = pltpu.SemaphoreType.DMA
    tree = pltpu.VMEM((device_bits, width // 2, BLK), BF16), pltpu.VMEM((device_bits, width // 4, BLK), BF16)
    table = level_table.transpose(1, 2, 0)
    results = pl.pallas_call(
        functools.partial(layer, seq_size, head_size, heads),
        out_shape=(
            *(pltpu.VMEM((tokens, width), F32),) * 3,
            *(pltpu.VMEM((tokens, width), BF16),) * 2,
            pltpu.VMEM((blocks, width, BLK), F32),
            pltpu.VMEM((device_bits, width, BLK), BF16),
        ),
        in_specs=[pl.BlockSpec(memory_space=pltpu.HBM)] * 5 + [vmem, pl.BlockSpec(memory_space=pltpu.HBM)],
        out_specs=(vmem,) * 7,
        scratch_shapes=[
            pltpu.VMEM((tokens, head_size * feats), BF16),
            pltpu.VMEM(w_out.shape, BF16),
            pltpu.VMEM((tokens, width), BF16),
            pltpu.VMEM((tokens, width), BF16),
            pltpu.VMEM((tokens, width), F32),
            pltpu.VMEM(table.shape, F32),
            pltpu.VMEM((levels * heads, table.shape[2]), F32),
            pltpu.VMEM((heads * levels, tokens), F32),
            pltpu.VMEM((tokens, BLK), F32),
            pltpu.VMEM((heads, (levels - 1) * BLK, tokens), BF16),
            pltpu.VMEM((blocks, width, BLK), BF16),
            pltpu.VMEM((blocks, width, BLK), F32),
            pltpu.VMEM((blocks, local_bits, width, BLK), BF16),
            pltpu.VMEM((width, BLK), BF16),
            *tree,
            pltpu.VMEM((device_bits, width, BLK), BF16),
            pltpu.VMEM((device_bits, width, BLK), BF16),
            pltpu.VMEM((device_bits, width, BLK), F32),
            *tree,
            dma((5,)),
            dma((3,)),
            dma((5,)),
            dma((head_size, blocks)),
            *[dma((device_bits,))] * 8,
        ],
        compiler_params=pltpu.CompilerParams(
            collective_id=0, has_side_effects=True, vmem_limit_bytes=54 * 2**20
        ),
        name="layer",
    )(grad_y, w_out, queries, keys, values, level_rows.reshape(1, tokens), table)

    return pl.pallas_call(
        finish,
        out_shape=(jax.ShapeDtypeStruct((tokens, width), F32),) * 3,
        in_specs=[vmem] * 7,
        out_specs=(hbm,) * 3,
        scratch_shapes=[pltpu.VMEM((tokens, width), F32)] * 2 + [dma((3 * blocks,))],
        compiler_params=pltpu.CompilerParams(vmem_limit_bytes=10 * 2**20),
        name="store",
    )(*[pltpu.with_memory_space_constraint(result, pltpu.VMEM) for result in results])


def solution(mesh):
    return jax.shard_map(
        shards,
        mesh=mesh,
        in_specs=(
            P("seq", "head"),
            P("head", None),
            P("seq", "head"),
            P("seq", "head"),
            P("seq", "head"),
            P("seq"),
            P(None, None, "head"),
        ),
        out_specs=(P("seq", "head"), P("seq", "head"), P("seq", "head")),
        check_vma=False,
    )
```
